256 devices in a mesh: dp: 32 (over x, y, core), proto: 8 (over z).
Axes of the slice: x: 4, y: 4, z: 8, core: 2. Of those that a mesh axis runs over, the one named last changes fastest.
Arguments:
- teacher_feats: bfloat16 [8192, 256], P('dp'), may hold values from -4 to 4
- student_feats: bfloat16 [8192, 256], P('dp'), may hold values from -4 to 4
- proto_weight: bfloat16 [256, 65536], P(None, 'proto'), may hold values from -1 to 1
- token_mask: int32 [8192], P('dp'), may hold values 0 or 1
Outputs:
- targets: bfloat16 [8192, 65536], P('dp', 'proto')
- weight_grad: float32 [256, 65536], P('dp', 'proto')
- feature_grad: float32 [8192, 256], P('dp', 'proto')
The draws below stay inside these ranges and needn't reach their ends.
All inputs are finite; a program needn't handle non-finite values. No bound on the sum of `token_mask` on one device may be relied on, other than what follows from the above.
Results may differ from the reference program's by a relative error of at most 0.0029.
Values sent between devices are 32-bit elements; how exact they have to be, the bound alone decides.
A program may use at most 128 MiB of HBM per device.

```python
import math
import jax
import jax.numpy as jnp
from jax import lax

D = 256
PROTOS = 65536
SWEEPS = 3
TOKENS = 8192


def proto_columns(key, power):
    normal_part = jnp.clip(jax.random.normal(key, (D, PROTOS), jnp.float32), -6.0, 6.0)
    return jnp.sign(normal_part) * jnp.abs(normal_part) ** power / jnp.sqrt(jnp.float32(D))


def scaled_rows(key, lowest, highest):
    keys_all = jax.random.split(key, 2)
    row_gain = jnp.exp(jax.random.uniform(keys_all[0], (TOKENS, 1), jnp.float32, jnp.log(lowest), jnp.log(highest)))
    return jnp.clip(jax.random.normal(keys_all[1], (TOKENS, D), jnp.float32), -6.0, 6.0) * row_gain


def draw_proto_weight(key, part):
    return proto_columns(key, 1.0).astype(jnp.bfloat16)


def draw_teacher_feats(key, part):
    key = jax.random.fold_in(key, 3)
    return jnp.clip(scaled_rows(key, 0.03, 0.3), -4.0, 4.0).astype(jnp.bfloat16)


def draw_student_feats(key, part):
    key = jax.random.fold_in(key, 5)
    return jnp.clip(scaled_rows(key, 0.03, 0.3), -4.0, 4.0).astype(jnp.bfloat16)


def set_ends(values, rng, low, high):
    longest = values.shape.index(max(values.shape))
    spots = []
    for shift in (0, 1):
        where = [jax.random.randint(jax.random.fold_in(rng, axis), (), 0, length) for axis, length in enumerate(values.shape)]
        where[longest] = (where[longest] + shift) % values.shape[longest]
        spots.append(tuple(where))
    return values.at[spots[0]].set(low).at[spots[1]].set(high)


def setup_inputs(seed: int = 0) -> dict:
    key_of = jax.random.split(jax.random.key(seed), 5)
    return {
        "teacher_feats": draw_teacher_feats(jax.random.fold_in(key_of[4], 71), 0),
        "student_feats": draw_student_feats(jax.random.fold_in(key_of[4], 71), 0),
        "proto_weight": draw_proto_weight(jax.random.fold_in(key_of[4], 71), 0),
        "token_mask": set_ends((jax.random.randint(key_of[3], (TOKENS,), 0, 2) < 1).astype(jnp.int32), jax.random.fold_in(key_of[3], 1), 0, 1),
    }


teacher_temp = 0.07
student_temp = 0.1


def reference(teacher_feats, student_feats, proto_weight, token_mask):
    live_rows = token_mask.astype(jnp.float32)
    teacher_logits = jnp.dot(teacher_feats, proto_weight, preferred_element_type=jnp.float32) / teacher_temp
    row_peak = jnp.max(teacher_logits, axis=1)
    expo_table = live_rows[:, None] * jnp.exp(teacher_logits - row_peak[:, None])
    token_scale = jnp.ones((TOKENS,), jnp.float32)
    proto_scale = jnp.ones((PROTOS,), jnp.float32)
    for sweep_index in range(SWEEPS):
        proto_scale = 1.0 / jnp.dot(token_scale, expo_table, precision=lax.Precision.HIGHEST)
        token_scale = 1.0 / (jnp.dot(expo_table, proto_scale, precision=lax.Precision.HIGHEST) + 1.0 - live_rows)
    block_rows = math.gcd(TOKENS, 512)
    block_count = TOKENS // block_rows
    inputs = (student_feats.reshape(block_count, block_rows, D),
              expo_table.reshape(block_count, block_rows, PROTOS),
              token_scale.reshape(block_count, block_rows),
              live_rows.reshape(block_count, block_rows))

    def step(grad_total, block):
        feats, expo, scale, alive = block
        target = scale[:, None] * expo * proto_scale[None, :]
        logits = jnp.dot(feats, proto_weight, preferred_element_type=jnp.float32) / student_temp
        peak = jnp.max(logits, axis=1)
        total = jnp.sum(jnp.exp(logits - peak[:, None]), axis=1)
        lse_rows = peak + jnp.log(total)
        delta = (alive[:, None] * (jnp.exp(logits - lse_rows[:, None]) - target)).astype(jnp.bfloat16)
        grad_total = grad_total + lax.dot_general(feats, delta, (((0,), (0,)), ((), ())), preferred_element_type=jnp.float32)
        feat_grad = lax.dot_general(delta, proto_weight, (((1,), (1,)), ((), ())), preferred_element_type=jnp.float32)
        return grad_total, (target.astype(jnp.bfloat16), feat_grad)

    grad_start = jnp.zeros((D, PROTOS), jnp.float32)
    weight_grad, outputs = lax.scan(step, grad_start, inputs)
    targets = outputs[0].reshape(TOKENS, PROTOS)
    feature_grad = outputs[1].reshape(TOKENS, D)
    return targets, weight_grad, feature_grad
```

```python
import math

import jax
import jax.numpy as jnp
from jax import lax
from jax.experimental import pallas as pl
from jax.experimental.pallas import tpu as pltpu
from jax.sharding import PartitionSpec as P

SWEEPS = 3
TEACHER = math.log2(math.e) / 0.07
STUDENT = math.log2(math.e) / 0.1
MESH = pl.DeviceIdType.MESH
NX, NY, NC, NZ = 4, 4, 2, 8
ROWS = 256
WIDE = 1024
BLOCKS = 8
TILES = WIDE // 128


def wait_all(ref, sem):
    pltpu.make_async_copy(ref, ref, sem).wait()


def to_rows(lanes):
    return jnp.transpose(jnp.broadcast_to(lanes, (128, ROWS)))


def kernel(
    tf_ref, sf_ref, mask_ref, w_hbm,
    out_hbm, weight_hbm, feature_ref,
    w, expo, soft, peak_b, acc, t_b, g_b, sft, tgt, wpart,
    col_tx, core_rx, x_tx, x_rx, y_tx, y_rx, p_ref,
    z_tx, z_rx, s_tx, s_rx,
    w_sem, out_sem, send, recv,
):
    dp = lax.axis_index("dp")
    z = lax.axis_index("proto")
    cx, cy, cc = dp // (NY * NC), lax.rem(dp // NC, NY), lax.rem(dp, NC)

    def at(x, y, c):
        return {"dp": (x * NY + y) * NC + c}

    partner = at(cx, cy, 1 - cc)
    x_peers = [at(lax.rem(cx + k, NX), cy, cc) for k in range(1, NX)]
    y_peers = [at(cx, lax.rem(cy + k, NY), cc) for k in range(1, NY)]
    z_peers = [{"proto": lax.rem(z + k, NZ)} for k in range(1, NZ)]

    barrier = pltpu.get_barrier_semaphore()
    peers = [partner] + x_peers + y_peers + z_peers
    for peer in peers:
        pl.semaphore_signal(barrier, inc=1, device_id=peer, device_id_type=MESH)

    def load(b):
        return pltpu.make_async_copy(
            w_hbm.at[:, pl.ds(pl.multiple_of(b * WIDE, WIDE), WIDE)], w.at[b], w_sem.at[b]
        )

    def start_load(b, c):
        load(b).start()
        return c

    lax.fori_loop(0, BLOCKS, start_load, 0)

    def push(src, dst, group, devices):
        for k, device in enumerate(devices):
            pltpu.make_async_remote_copy(
                src_ref=src, dst_ref=dst.at[k], send_sem=send.at[group], recv_sem=recv.at[group],
                device_id=device, device_id_type=MESH,
            ).start()

    def logits(feats_ref, table, first):
        acc[...] = jnp.full(acc.shape, -jnp.inf, jnp.float32)

        def block(b, c):
            if first:
                load(b).wait()
            for s in range(WIDE // 256):
                part = jnp.dot(
                    feats_ref[...], w[b, :, s * 256:(s + 1) * 256],
                    preferred_element_type=jnp.float32,
                )
                table[b, :, s * 256:(s + 1) * 256] = part
                acc[...] = jnp.maximum(acc[...], jnp.maximum(part[:, :128], part[:, 128:]))
            return c

        lax.fori_loop(0, BLOCKS, block, 0)
        peak_b[...] = jnp.broadcast_to(jnp.max(acc[...], axis=1, keepdims=True), acc.shape)
        return jnp.max(jnp.transpose(acc[...]), axis=0, keepdims=True)

    def powers(table, scale, low, high, total):
        def block(b, c):
            for s in range(TILES):
                at_s = (b, slice(None), slice(s * 128, (s + 1) * 128))
                value = jnp.exp2((table[at_s] - peak_b[...]) * scale)
                table[at_s] = value
                if total:
                    acc[...] += value
            return c

        lax.fori_loop(low, high, block, 0)

    def row_sum():
        return jnp.sum(jnp.transpose(acc[...]), axis=0, keepdims=True)

    live = mask_ref[...].astype(jnp.float32)

    local_peak = logits(tf_ref, expo, True)
    z_tx[0] = local_peak
    pl.semaphore_wait(barrier, len(peers))
    push(z_tx.at[0], z_rx.at[0], 0, z_peers)
    powers(expo, TEACHER, 0, BLOCKS, False)
    sft[...] = jnp.transpose(sf_ref[...])
    wait_all(z_rx.at[0], recv.at[0])
    joint_peak = jnp.maximum(jnp.max(z_rx[0], axis=0), local_peak)
    factor = live * jnp.exp2((local_peak - joint_peak) * TEACHER)
    t_b[...] = to_rows(factor)

    for sweep in range(SWEEPS):
        base = 2 + 5 * sweep

        def column_block(b, c):
            for s in range(TILES):
                col = expo[b, :, s * 128:(s + 1) * 128] * t_b[...]
                col_tx[pl.ds(b * TILES + s, 1), :] = jnp.sum(col, axis=0, keepdims=True)
            return c

        lax.fori_loop(0, BLOCKS, column_block, 0)
        half = BLOCKS * TILES // 2
        mine = pl.ds(pl.multiple_of(cc * half, half), half)
        other = pl.ds(pl.multiple_of((1 - cc) * half, half), half)
        push(col_tx.at[other], core_rx.at[sweep], base, [partner])
        wait_all(core_rx.at[sweep], recv.at[base])
        x_sum = col_tx[mine, :] + core_rx[sweep, 0]
        x_tx[sweep] = x_sum
        push(x_tx.at[sweep], x_rx.at[sweep], base + 1, x_peers)
        if sweep == 0:
            student_peak = logits(sf_ref, soft, False)
        wait_all(x_rx.at[sweep], recv.at[base + 1])
        y_sum = x_sum + jnp.sum(x_rx[sweep], axis=0)
        y_tx[sweep] = y_sum
        push(y_tx.at[sweep], y_rx.at[sweep], base + 2, y_peers)
        if sweep == 0:
            acc[...] = jnp.zeros(acc.shape, jnp.float32)
            powers(soft, STUDENT, 0, BLOCKS, True)
            student_total = row_sum()
            s_tx[0:1] = student_peak
            s_tx[1:2] = student_total
            push(s_tx, s_rx, 1, z_peers)
        wait_all(y_rx.at[sweep], recv.at[base + 2])
        p_half = 1.0 / (y_sum + jnp.sum(y_rx[sweep], axis=0))
        p_ref[sweep, mine, :] = p_half
        pltpu.make_async_remote_copy(
            src_ref=p_ref.at[sweep, mine], dst_ref=p_ref.at[sweep, mine],
            send_sem=send.at[base + 3], recv_sem=recv.at[base + 3],
            device_id=partner, device_id_type=MESH,
        ).start()
        wait_all(p_ref.at[sweep, other], recv.at[base + 3])

        acc[...] = jnp.zeros(acc.shape, jnp.float32)

        def row_block(b, c):
            part = acc[...]
            for s in range(TILES):
                part += expo[b, :, s * 128:(s + 1) * 128] * p_ref[sweep, pl.ds(b * TILES + s, 1), :]
            acc[...] = part
            return c

        lax.fori_loop(0, BLOCKS, row_block, 0)
        local_row = row_sum() * factor
        z_tx[1 + sweep] = local_row
        push(z_tx.at[1 + sweep], z_rx.at[1 + sweep], base + 4, z_peers)
        if sweep == SWEEPS - 1:
            wait_all(s_rx, recv.at[1])
            top = jnp.maximum(jnp.max(s_rx[:, 0:1], axis=0), student_peak)
            total = student_total * jnp.exp2((student_peak - top) * STUDENT)
            for k in range(NZ - 1):
                total += s_rx[k, 1:2] * jnp.exp2((s_rx[k, 0:1] - top) * STUDENT)
            g_b[...] = to_rows(live * jnp.exp2((student_peak - top) * STUDENT) / total)
        wait_all(z_rx.at[1 + sweep], recv.at[base + 4])
        row = local_row + jnp.sum(z_rx[1 + sweep], axis=0)
        t_b[...] = to_rows(factor / (row + (1.0 - live)))
        wait_all(core_rx.at[sweep], send.at[base])
        wait_all(x_rx.at[sweep], send.at[base + 1])
        wait_all(y_rx.at[sweep], send.at[base + 2])
        wait_all(p_ref.at[sweep, other], send.at[base + 3])
        wait_all(z_rx.at[1 + sweep], send.at[base + 4])
    wait_all(z_rx.at[0], send.at[0])
    wait_all(s_rx, send.at[1])

    def store(b):
        span = pl.ds(pl.multiple_of(b * WIDE, WIDE), WIDE)
        return (
            pltpu.make_async_copy(tgt.at[b], out_hbm.at[:, span], out_sem.at[0, b]),
            pltpu.make_async_copy(wpart.at[b], weight_hbm.at[:, span], out_sem.at[1, b]),
        )

    feature_ref[...] = jnp.zeros(feature_ref.shape, jnp.float32)

    def final_block(b, c):
        for s in range(WIDE // 256):
            halves = []
            for h in range(2):
                lanes = slice(s * 256 + h * 128, s * 256 + (h + 1) * 128)
                target = expo[b, :, lanes] * t_b[...] * p_ref[
                    SWEEPS - 1, pl.ds(b * TILES + s * 2 + h, 1), :]
                tgt[b, :, lanes] = target.astype(jnp.bfloat16)
                halves.append((soft[b, :, lanes] * g_b[...] - target).astype(jnp.bfloat16))
            delta = jnp.concatenate(halves, axis=1)
            span = slice(s * 256, (s + 1) * 256)
            feature_ref[...] += lax.dot_general(
                delta, w[b, :, span], (((1,), (1,)), ((), ())), preferred_element_type=jnp.float32
            )
            wpart[b, :, span] = jnp.dot(sft[...], delta, preferred_element_type=jnp.float32)
        for copy in store(b):
            copy.start()
        return c

    lax.fori_loop(0, BLOCKS, final_block, 0)

    def drain(b, c):
        for copy in store(b):
            copy.wait()
        return c

    lax.fori_loop(0, BLOCKS, drain, 0)


def fused(tf, sf, mask, w):
    d, protos = w.shape
    f32, bf16 = jnp.float32, jnp.bfloat16
    vec = BLOCKS * TILES
    groups = 2 + 5 * SWEEPS
    table = pltpu.VMEM((BLOCKS, ROWS, WIDE), f32)
    rows = pltpu.VMEM((ROWS, 128), f32)
    return pl.pallas_call(
        kernel,
        out_shape=(
            jax.ShapeDtypeStruct((ROWS, protos), bf16),
            jax.ShapeDtypeStruct((d, protos), f32),
            jax.ShapeDtypeStruct((ROWS, d), f32),
        ),
        in_specs=[pl.BlockSpec(memory_space=pltpu.VMEM)] * 3 + [pl.BlockSpec(memory_space=pl.ANY)],
        out_specs=(
            pl.BlockSpec(memory_space=pl.ANY),
            pl.BlockSpec(memory_space=pl.ANY),
            pl.BlockSpec(memory_space=pltpu.VMEM),
        ),
        scratch_shapes=[
            pltpu.VMEM((BLOCKS, d, WIDE), bf16),
            table, table, rows, rows, rows, rows,
            pltpu.VMEM((d, ROWS), bf16),
            pltpu.VMEM((BLOCKS, ROWS, WIDE), bf16),
            pltpu.VMEM((BLOCKS, d, WIDE), f32),
            pltpu.VMEM((vec, 128), f32),
            pltpu.VMEM((SWEEPS, 1, vec // 2, 128), f32),
            pltpu.VMEM((SWEEPS, vec // 2, 128), f32),
            pltpu.VMEM((SWEEPS, NX - 1, vec // 2, 128), f32),
            pltpu.VMEM((SWEEPS, vec // 2, 128), f32),
            pltpu.VMEM((SWEEPS, NY - 1, vec // 2, 128), f32),
            pltpu.VMEM((SWEEPS, vec, 128), f32),
            pltpu.VMEM((SWEEPS + 1, 1, ROWS), f32),
            pltpu.VMEM((SWEEPS + 1, NZ - 1, 1, ROWS), f32),
            pltpu.VMEM((2, ROWS), f32),
            pltpu.VMEM((NZ - 1, 2, ROWS), f32),
            pltpu.SemaphoreType.DMA((BLOCKS,)),
            pltpu.SemaphoreType.DMA((2, BLOCKS)),
            pltpu.SemaphoreType.DMA((groups,)),
            pltpu.SemaphoreType.DMA((groups,)),
        ],
        compiler_params=pltpu.CompilerParams(
            collective_id=0, has_side_effects=True, vmem_limit_bytes=56 * 2**20
        ),
        name="sinkhorn",
    )(tf, sf, mask, w)


def on_device(teacher_feats, student_feats, proto_weight, token_mask):
    targets, weight_part, feature_part = fused(
        teacher_feats, student_feats, token_mask.reshape(1, -1), proto_weight
    )
    feature_grad = lax.psum_scatter(feature_part, "proto", scatter_dimension=1, tiled=True)
    weight_grad = lax.psum_scatter(weight_part, "dp", scatter_dimension=0, tiled=True)
    return targets, weight_grad, feature_grad


def solution(mesh):
    placed = (P("dp", None), P("dp", None), P(None, "proto"), P("dp"))
    return jax.shard_map(
        on_device,
        mesh=mesh,
        in_specs=placed,
        out_specs=(P("dp", "proto"), P("dp", "proto"), P("dp", "proto")),
        check_vma=False,
    )
```

```python
import math

import jax
import jax.numpy as jnp
from jax import lax
from jax.experimental import pallas as pl
from jax.experimental.pallas import tpu as pltpu
from jax.sharding import PartitionSpec as P

SWEEPS = 3
TEACHER = math.log2(math.e) / 0.07
STUDENT = math.log2(math.e) / 0.1
MESH = pl.DeviceIdType.MESH
NX, NY, NC, NZ = 4, 4, 2, 8
ROWS = 256
WIDE = 1024
BLOCKS = 8
TILES = WIDE // 128
PARTS = WIDE // 256
NT = (((1,), (1,)), ((), ()))
BASE = 8
PEAK, TOTALS, FEATS, RELAY, SCALARS, TOKENS, FEATURE, SPREAD = range(BASE)
RS = BASE + 5 * SWEEPS


def wait_all(ref, sem):
    pltpu.make_async_copy(ref, ref, sem).wait()


def to_rows(lanes, width=ROWS):
    return jnp.transpose(jnp.broadcast_to(lanes, (128, width)))


def kernel(
    tf_ref, sf_ref, mask_ref, w_hbm,
    out_hbm, weight_ref, feature_ref,
    w, expo, soft, peak_b, acc, t_b, g_b, tgt, delta_a, fpt, f_rx,
    wt, eb, qb, gall, sft, dcat, pcol, scal, tall, wp_tx, rs_rx, a_tx, a_rx,
    col_tx, core_rx, x_tx, x_rx, y_tx, y_rx, p_ref,
    z_tx, z_rx, s_tx, s_rx,
    w_sem, out_sem, send, recv,
):
    dp = lax.axis_index("dp")
    z = lax.axis_index("proto")
    cx, cy, cc = dp // (NY * NC), lax.rem(dp // NC, NY), lax.rem(dp, NC)

    def at(x, y, c):
        return {"dp": (x * NY + y) * NC + c}

    def row_place(n):
        x = lax.rem(cx + n % NX, NX)
        return x, (cc if n < NX else 1 - cc)

    def row_source(n):
        x = lax.rem(cx + NX - n % NX, NX)
        return x * NC + (cc if n < NX else 1 - cc)

    partner = at(cx, cy, 1 - cc)
    row_peers = [at(row_place(n)[0], cy, row_place(n)[1]) for n in range(1, BLOCKS)]
    x_peers = row_peers[: NX - 1]
    y_peers = [at(cx, lax.rem(cy + k, NY), cc) for k in range(1, NY)]
    z_place = [lax.rem(z + k, NZ) for k in range(1, NZ)]
    z_peers = [{"proto": place} for place in z_place]
    mine_g = cx * NC + cc

    barrier = pltpu.get_barrier_semaphore()
    peers = row_peers + y_peers + z_peers
    for peer in peers:
        pl.semaphore_signal(barrier, inc=1, device_id=peer, device_id_type=MESH)

    def load(b):
        return pltpu.make_async_copy(
            w_hbm.at[:, pl.ds(pl.multiple_of(b * WIDE, WIDE), WIDE)], w.at[b], w_sem.at[b]
        )

    def start_load(b, c):
        load(b).start()
        return c

    lax.fori_loop(0, BLOCKS, start_load, 0)

    def send_one(src, dst, group, device):
        pltpu.make_async_remote_copy(
            src_ref=src, dst_ref=dst, send_sem=send.at[group], recv_sem=recv.at[group],
            device_id=device, device_id_type=MESH,
        ).start()

    def push(src, dst, group, devices):
        for k, device in enumerate(devices):
            send_one(src, dst.at[k], group, device)

    def logits(feats_ref, table, first):
        acc[...] = jnp.full(acc.shape, -jnp.inf, jnp.float32)

        def block(b, c):
            if first:
                load(b).wait()
            for s in range(PARTS):
                part = jnp.dot(
                    feats_ref[...], w[b, :, s * 256:(s + 1) * 256],
                    preferred_element_type=jnp.float32,
                )
                table[b, :, s * 256:(s + 1) * 256] = part
                acc[...] = jnp.maximum(acc[...], jnp.maximum(part[:, :128], part[:, 128:]))
            return c

        lax.fori_loop(0, BLOCKS, block, 0)
        peak_b[...] = jnp.broadcast_to(jnp.max(acc[...], axis=1, keepdims=True), acc.shape)
        return jnp.max(jnp.transpose(acc[...]), axis=0, keepdims=True)

    def powers(table, scale, total):
        def block(b, c):
            for s in range(TILES):
                at_s = (b, slice(None), slice(s * 128, (s + 1) * 128))
                value = jnp.exp2((table[at_s] - peak_b[...]) * scale)
                table[at_s] = value
                if total:
                    acc[...] += value
            return c

        lax.fori_loop(0, BLOCKS, block, 0)

    def row_sum():
        return jnp.sum(jnp.transpose(acc[...]), axis=0, keepdims=True)

    def shared_tables(n, c):
        feats_t = gall[n, 0].astype(jnp.bfloat16)
        feats_s = gall[n, 1].astype(jnp.bfloat16)
        sft[:, pl.ds(pl.multiple_of(n * ROWS, ROWS), ROWS)] = feats_s
        for q in range(PARTS):
            rows = slice(q * 256, (q + 1) * 256)
            dot = jnp.dot(wt[rows, :], feats_t, preferred_element_type=jnp.float32)
            eb[n, rows, :] = jnp.exp2((dot - scal[n, 0:1]) * TEACHER)
            dot = jnp.dot(wt[rows, :], feats_s, preferred_element_type=jnp.float32)
            qb[n, rows, :] = jnp.exp2((dot - scal[n, 1:2]) * STUDENT) * scal[n, 2:3]
        return c

    live = mask_ref[...].astype(jnp.float32)

    local_peak = logits(tf_ref, expo, True)
    z_tx[0] = local_peak
    gall[0, 0] = jnp.transpose(tf_ref[...].astype(jnp.float32))
    gall[0, 1] = jnp.transpose(sf_ref[...].astype(jnp.float32))
    pl.semaphore_wait(barrier, len(peers))
    push(z_tx.at[0], z_rx.at[0], PEAK, z_peers)
    for n in range(1, NX):
        send_one(gall.at[0], gall.at[n], FEATS, x_peers[n - 1])
    send_one(gall.at[0], gall.at[NX], RELAY, partner)
    powers(expo, TEACHER, False)
    wait_all(z_rx.at[0], recv.at[PEAK])
    joint_peak = jnp.maximum(jnp.max(z_rx[0], axis=0), local_peak)
    factor = live * jnp.exp2((local_peak - joint_peak) * TEACHER)
    t_b[...] = to_rows(factor)

    for sweep in range(SWEEPS):
        base = BASE + 5 * sweep

        def column_block(b, c):
            for s in range(TILES):
                col = expo[b, :, s * 128:(s + 1) * 128] * t_b[...]
                col_tx[pl.ds(b * TILES + s, 1), :] = jnp.sum(col, axis=0, keepdims=True)
            return c

        lax.fori_loop(0, BLOCKS, column_block, 0)
        half = BLOCKS * TILES // 2
        mine = pl.ds(pl.multiple_of(cc * half, half), half)
        other = pl.ds(pl.multiple_of((1 - cc) * half, half), half)
        push(col_tx.at[other], core_rx.at[sweep], base, [partner])
        wait_all(core_rx.at[sweep], recv.at[base])
        x_sum = col_tx[mine, :] + core_rx[sweep, 0]
        x_tx[sweep] = x_sum
        push(x_tx.at[sweep], x_rx.at[sweep], base + 1, x_peers)
        if sweep == 0:
            student_peak = logits(sf_ref, soft, False)
        if sweep == 1:
            wait_all(gall.at[pl.ds(1, NX - 1)], recv.at[FEATS])
            for n in range(1, NX):
                send_one(gall.at[n], gall.at[NX + n], RELAY, partner)
        if sweep == 2:
            lax.fori_loop(NX, BLOCKS, shared_tables, 0)
        wait_all(x_rx.at[sweep], recv.at[base + 1])
        y_sum = x_sum + jnp.sum(x_rx[sweep], axis=0)
        y_tx[sweep] = y_sum
        push(y_tx.at[sweep], y_rx.at[sweep], base + 2, y_peers)
        if sweep == 0:
            acc[...] = jnp.zeros(acc.shape, jnp.float32)
            powers(soft, STUDENT, True)
            student_total = row_sum()
            s_tx[0:1] = student_peak
            s_tx[1:2] = student_total
            push(s_tx, s_rx, TOTALS, z_peers)
        if sweep == 1:
            wait_all(scal.at[pl.ds(1, BLOCKS - 1)], recv.at[SCALARS])
            lax.fori_loop(0, 2, shared_tables, 0)
        wait_all(y_rx.at[sweep], recv.at[base + 2])
        p_half = 1.0 / (y_sum + jnp.sum(y_rx[sweep], axis=0))
        p_ref[sweep, mine, :] = p_half
        send_one(p_ref.at[sweep, mine], p_ref.at[sweep, mine], base + 3, partner)
        wait_all(p_ref.at[sweep, other], recv.at[base + 3])

        acc[...] = jnp.zeros(acc.shape, jnp.float32)

        def row_block(b, c):
            part = acc[...]
            for s in range(TILES):
                part += expo[b, :, s * 128:(s + 1) * 128] * p_ref[sweep, pl.ds(b * TILES + s, 1), :]
            acc[...] = part
            return c

        lax.fori_loop(0, BLOCKS, row_block, 0)
        local_row = row_sum() * factor
        z_tx[1 + sweep] = local_row
        push(z_tx.at[1 + sweep], z_rx.at[1 + sweep], base + 4, z_peers)
        if sweep == 0:
            wt[...] = jnp.transpose(w[mine_g])
            wait_all(s_rx, recv.at[TOTALS])
            top = jnp.maximum(jnp.max(s_rx[:, 0:1], axis=0), student_peak)
            total = student_total * jnp.exp2((student_peak - top) * STUDENT)
            for k in range(NZ - 1):
                total += s_rx[k, 1:2] * jnp.exp2((s_rx[k, 0:1] - top) * STUDENT)
            share = live * jnp.exp2((student_peak - top) * STUDENT) / total
            g_b[...] = to_rows(share)
            scal[0, 0:1] = local_peak
            scal[0, 1:2] = student_peak
            scal[0, 2:3] = share
            for n in range(1, BLOCKS):
                send_one(scal.at[0], scal.at[n], SCALARS, row_peers[n - 1])
        if sweep == 1:
            lax.fori_loop(2, NX, shared_tables, 0)
            wait_all(gall.at[pl.ds(NX, NX)], recv.at[RELAY])
        if sweep == SWEEPS - 1:
            for s in range(TILES):
                pcol[s * 128:(s + 1) * 128, :] = to_rows(
                    p_ref[sweep, pl.ds(mine_g * TILES + s, 1), :], 128)
        wait_all(z_rx.at[1 + sweep], recv.at[base + 4])
        row = local_row + jnp.sum(z_rx[1 + sweep], axis=0)
        scale = factor / (row + (1.0 - live))
        if sweep == SWEEPS - 1:
            tall[0] = scale
            for n in range(1, BLOCKS):
                send_one(tall.at[0], tall.at[n], TOKENS, row_peers[n - 1])
        t_b[...] = to_rows(scale)
        wait_all(core_rx.at[sweep], send.at[base])
        wait_all(x_rx.at[sweep], send.at[base + 1])
        wait_all(y_rx.at[sweep], send.at[base + 2])
        wait_all(p_ref.at[sweep, other], send.at[base + 3])
        wait_all(z_rx.at[1 + sweep], send.at[base + 4])

    def store(b):
        span = pl.ds(pl.multiple_of(b * WIDE, WIDE), WIDE)
        return pltpu.make_async_copy(tgt.at[b], out_hbm.at[:, span], out_sem.at[b])

    fpt[...] = jnp.zeros(fpt.shape, jnp.float32)

    def own_block(b, c):
        for s in range(TILES):
            lanes = slice(s * 128, (s + 1) * 128)
            target = expo[b, :, lanes] * t_b[...] * p_ref[SWEEPS - 1, pl.ds(b * TILES + s, 1), :]
            tgt[b, :, lanes] = target.astype(jnp.bfloat16)
            delta_a[:, lanes] = (soft[b, :, lanes] * g_b[...] - target).astype(jnp.bfloat16)
        fpt[...] += lax.dot_general(
            w[b], delta_a[...], NT, preferred_element_type=jnp.float32
        ).reshape(fpt.shape)
        store(b).start()
        return c

    def shared_part(q, c):
        rows = pl.ds(pl.multiple_of(q * 256, 256), 256)
        for n in range(BLOCKS):
            for h in range(2):
                lanes = slice(h * 128, (h + 1) * 128)
                target = eb[n, rows, lanes] * pcol[rows, :] * tall[n, :, lanes]
                dcat[:, n * ROWS + h * 128:n * ROWS + (h + 1) * 128] = (
                    qb[n, rows, lanes] - target).astype(jnp.bfloat16)
        grad = lax.dot_general(sft[...], dcat[...], NT, preferred_element_type=jnp.float32)
        for x in range(NX):
            for y in range(NY):
                top = (x * NY + y) * 16
                wp_tx[q, y, x * 16:(x + 1) * 16, :] = grad[top:top + 16]
        for k in range(1, NY):
            send_one(wp_tx.at[q, lax.rem(cy + k, NY)], rs_rx.at[q, k - 1], RS + q, y_peers[k - 1])
        return c

    lax.fori_loop(0, BLOCKS // 2, own_block, 0)
    wait_all(tall.at[pl.ds(1, BLOCKS - 1)], recv.at[TOKENS])
    lax.fori_loop(0, PARTS, shared_part, 0)
    lax.fori_loop(BLOCKS // 2, BLOCKS, own_block, 0)
    for k in range(1, NZ):
        send_one(fpt.at[z_place[k - 1]], f_rx.at[k - 1], FEATURE, z_peers[k - 1])

    def collect(q, c):
        wait_all(rs_rx.at[q], recv.at[RS + q])
        grad = wp_tx[q, cy] + jnp.sum(rs_rx[q], axis=0)
        a_tx[q] = grad.reshape(BLOCKS, 8, 256)
        for n in range(1, BLOCKS):
            x, core = row_place(n)
            send_one(a_tx.at[q, x * NC + core], a_rx.at[q, n - 1], SPREAD, row_peers[n - 1])
        return c

    lax.fori_loop(0, PARTS, collect, 0)
    wait_all(f_rx, recv.at[FEATURE])
    feature_ref[...] = jnp.transpose(fpt[z] + jnp.sum(f_rx[...], axis=0))
    wait_all(a_rx, recv.at[SPREAD])
    for q in range(PARTS):
        for n in range(BLOCKS):
            span = pl.ds(pl.multiple_of(row_source(n) * WIDE + q * 256, 256), 256)
            weight_ref[:, span] = a_rx[q, n - 1] if n else a_tx[q, mine_g]

    def drain(b, c):
        store(b).wait()
        return c

    lax.fori_loop(0, BLOCKS, drain, 0)
    wait_all(z_rx.at[0], send.at[PEAK])
    wait_all(s_rx, send.at[TOTALS])
    wait_all(gall.at[pl.ds(1, NX - 1)], send.at[FEATS])
    wait_all(gall.at[pl.ds(NX, NX)], send.at[RELAY])
    wait_all(scal.at[pl.ds(1, BLOCKS - 1)], send.at[SCALARS])
    wait_all(tall.at[pl.ds(1, BLOCKS - 1)], send.at[TOKENS])
    wait_all(f_rx, send.at[FEATURE])
    wait_all(a_rx, send.at[SPREAD])
    for q in range(PARTS):
        wait_all(rs_rx.at[q], send.at[RS + q])


def on_device(teacher_feats, student_feats, proto_weight, token_mask):
    d, protos = proto_weight.shape
    f32, bf16 = jnp.float32, jnp.bfloat16
    vec = BLOCKS * TILES
    groups = RS + PARTS
    table = pltpu.VMEM((BLOCKS, ROWS, WIDE), f32)
    shared = pltpu.VMEM((BLOCKS, WIDE, ROWS), f32)
    rows = pltpu.VMEM((ROWS, 128), f32)
    vmem = pl.BlockSpec(memory_space=pltpu.VMEM)
    hbm = pl.BlockSpec(memory_space=pl.ANY)
    return pl.pallas_call(
        kernel,
        out_shape=(
            jax.ShapeDtypeStruct((ROWS, protos), bf16),
            jax.ShapeDtypeStruct((d // (NX * NY * NC), protos), f32),
            jax.ShapeDtypeStruct((ROWS, d // NZ), f32),
        ),
        in_specs=[vmem, vmem, vmem, hbm],
        out_specs=(hbm, vmem, vmem),
        scratch_shapes=[
            pltpu.VMEM((BLOCKS, d, WIDE), bf16),
            table, table, rows, rows, rows, rows,
            pltpu.VMEM((BLOCKS, ROWS, WIDE), bf16),
            pltpu.VMEM((ROWS, WIDE), bf16),
            pltpu.VMEM((NZ, d // NZ, ROWS), f32),
            pltpu.VMEM((NZ - 1, d // NZ, ROWS), f32),
            pltpu.VMEM((WIDE, d), bf16),
            shared, shared,
            pltpu.VMEM((BLOCKS, 2, d, ROWS), f32),
            pltpu.VMEM((d, BLOCKS * ROWS), bf16),
            pltpu.VMEM((256, BLOCKS * ROWS), bf16),
            pltpu.VMEM((WIDE, 128), f32),
            pltpu.VMEM((BLOCKS, 3, ROWS), f32),
            pltpu.VMEM((BLOCKS, 1, ROWS), f32),
            pltpu.VMEM((PARTS, NY, d // NY, 256), f32),
            pltpu.VMEM((PARTS, NY - 1, d // NY, 256), f32),
            pltpu.VMEM((PARTS, BLOCKS, 8, 256), f32),
            pltpu.VMEM((PARTS, BLOCKS - 1, 8, 256), f32),
            pltpu.VMEM((vec, 128), f32),
            pltpu.VMEM((SWEEPS, 1, vec // 2, 128), f32),
            pltpu.VMEM((SWEEPS, vec // 2, 128), f32),
            pltpu.VMEM((SWEEPS, NX - 1, vec // 2, 128), f32),
            pltpu.VMEM((SWEEPS, vec // 2, 128), f32),
            pltpu.VMEM((SWEEPS, NY - 1, vec // 2, 128), f32),
            pltpu.VMEM((SWEEPS, vec, 128), f32),
            pltpu.VMEM((SWEEPS + 1, 1, ROWS), f32),
            pltpu.VMEM((SWEEPS + 1, NZ - 1, 1, ROWS), f32),
            pltpu.VMEM((2, ROWS), f32),
            pltpu.VMEM((NZ - 1, 2, ROWS), f32),
            pltpu.SemaphoreType.DMA((BLOCKS,)),
            pltpu.SemaphoreType.DMA((BLOCKS,)),
            pltpu.SemaphoreType.DMA((groups,)),
            pltpu.SemaphoreType.DMA((groups,)),
        ],
        compiler_params=pltpu.CompilerParams(
            collective_id=0, has_side_effects=True, vmem_limit_bytes=60 * 2**20
        ),
        name="sinkhorn",
    )(teacher_feats, student_feats, token_mask.reshape(1, -1), proto_weight)


def solution(mesh):
    placed = (P("dp", None), P("dp", None), P(None, "proto"), P("dp"))
    return jax.shard_map(
        on_device,
        mesh=mesh,
        in_specs=placed,
        out_specs=(P("dp", "proto"), P("dp", "proto"), P("dp", "proto")),
        check_vma=False,
    )
```

```python
import math

import jax
import jax.numpy as jnp
from jax import lax
from jax.experimental import pallas as pl
from jax.experimental.pallas import tpu as pltpu
from jax.sharding import PartitionSpec as P

SWEEPS = 3
TEACHER = math.log2(math.e) / 0.07
STUDENT = math.log2(math.e) / 0.1
MESH = pl.DeviceIdType.MESH
NX, NY, NC, NZ = 4, 4, 2, 8
ROWS = 256
WIDE = 1024
BLOCKS = 8
TILES = WIDE // 128
PARTS = WIDE // 256
NT = (((1,), (1,)), ((), ()))
BASE = 8
PEAK, TOTALS, FEATS, RELAY, SCALARS, TOKENS, FEATURE, SPREAD = range(BASE)
RS = BASE + 5 * SWEEPS


def wait_all(ref, sem):
    pltpu.make_async_copy(ref, ref, sem).wait()


def to_rows(lanes, width=ROWS):
    return jnp.transpose(jnp.broadcast_to(lanes, (128, width)))


def kernel(
    tf_ref, sf_ref, mask_ref, w_hbm,
    tgt, weight_ref, feature_ref,
    w, expo, soft, peak_b, acc, t_b, g_b, delta_a, fpt, f_rx,
    wt, eb, qb, gall, sft, dcat, pcol, scal, tall, wp_tx, rs_rx, a_tx, a_rx,
    col_tx, core_rx, x_tx, x_rx, y_tx, y_rx, p_ref,
    z_tx, z_rx, s_tx, s_rx,
    w_sem, send, recv,
):
    dp = lax.axis_index("dp")
    z = lax.axis_index("proto")
    cx, cy, cc = dp // (NY * NC), lax.rem(dp // NC, NY), lax.rem(dp, NC)

    def at(x, y, c):
        return {"dp": (x * NY + y) * NC + c}

    def row_place(n):
        x = lax.rem(cx + n % NX, NX)
        return x, (cc if n < NX else 1 - cc)

    def row_source(n):
        x = lax.rem(cx + NX - n % NX, NX)
        return x * NC + (cc if n < NX else 1 - cc)

    partner = at(cx, cy, 1 - cc)
    row_peers = [at(row_place(n)[0], cy, row_place(n)[1]) for n in range(1, BLOCKS)]
    x_peers = row_peers[: NX - 1]
    y_peers = [at(cx, lax.rem(cy + k, NY), cc) for k in range(1, NY)]
    z_place = [lax.rem(z + k, NZ) for k in range(1, NZ)]
    z_peers = [{"proto": place} for place in z_place]
    mine_g = cx * NC + cc

    barrier = pltpu.get_barrier_semaphore()
    peers = row_peers + y_peers + z_peers
    for peer in peers:
        pl.semaphore_signal(barrier, inc=1, device_id=peer, device_id_type=MESH)

    def load(b):
        return pltpu.make_async_copy(
            w_hbm.at[:, pl.ds(pl.multiple_of(b * WIDE, WIDE), WIDE)], w.at[b], w_sem.at[b]
        )

    def start_load(b, c):
        load(b).start()
        return c

    lax.fori_loop(0, BLOCKS, start_load, 0)

    def send_one(src, dst, group, device):
        pltpu.make_async_remote_copy(
            src_ref=src, dst_ref=dst, send_sem=send.at[group], recv_sem=recv.at[group],
            device_id=device, device_id_type=MESH,
        ).start()

    def push(src, dst, group, devices):
        for k, device in enumerate(devices):
            send_one(src, dst.at[k], group, device)

    def gather(first, last):
        def piece(q, c):
            for n in range(1, NX):
                at_q = (q // 4, pl.ds(pl.multiple_of(q % 4 * 64, 64), 64))
                send_one(gall.at[(0,) + at_q], gall.at[(n,) + at_q], FEATS, x_peers[n - 1])
            return c

        lax.fori_loop(first, last, piece, 0)

    def logits(feats_ref, table, first):
        acc[...] = jnp.full(acc.shape, -jnp.inf, jnp.float32)

        def block(b, c):
            if first:
                load(b).wait()
            for s in range(PARTS):
                part = jnp.dot(
                    feats_ref[...], w[b, :, s * 256:(s + 1) * 256],
                    preferred_element_type=jnp.float32,
                )
                table[b, :, s * 256:(s + 1) * 256] = part
                acc[...] = jnp.maximum(acc[...], jnp.maximum(part[:, :128], part[:, 128:]))
            return c

        lax.fori_loop(0, BLOCKS, block, 0)
        peak_b[...] = jnp.broadcast_to(jnp.max(acc[...], axis=1, keepdims=True), acc.shape)
        return jnp.max(jnp.transpose(acc[...]), axis=0, keepdims=True)

    def powers(table, scale, total):
        def block(b, c):
            for s in range(TILES):
                at_s = (b, slice(None), slice(s * 128, (s + 1) * 128))
                value = jnp.exp2((table[at_s] - peak_b[...]) * scale)
                table[at_s] = value
                if total:
                    acc[...] += value
            return c

        lax.fori_loop(0, BLOCKS, block, 0)

    def row_sum():
        return jnp.sum(jnp.transpose(acc[...]), axis=0, keepdims=True)

    def shared_tables(n, c):
        feats_t = gall[n, 0].astype(jnp.bfloat16)
        feats_s = gall[n, 1].astype(jnp.bfloat16)
        sft[:, pl.ds(pl.multiple_of(n * ROWS, ROWS), ROWS)] = feats_s
        for q in range(PARTS):
            rows = slice(q * 256, (q + 1) * 256)
            dot = jnp.dot(wt[rows, :], feats_t, preferred_element_type=jnp.float32)
            eb[n, rows, :] = jnp.exp2((dot - scal[n, 0:1]) * TEACHER)
            dot = jnp.dot(wt[rows, :], feats_s, preferred_element_type=jnp.float32)
            qb[n, rows, :] = jnp.exp2((dot - scal[n, 1:2]) * STUDENT) * scal[n, 2:3]
        return c

    live = mask_ref[...].astype(jnp.float32)

    local_peak = logits(tf_ref, expo, True)
    z_tx[0] = local_peak
    gall[0, 0] = jnp.transpose(tf_ref[...].astype(jnp.float32))
    gall[0, 1] = jnp.transpose(sf_ref[...].astype(jnp.float32))
    pl.semaphore_wait(barrier, len(peers))
    push(z_tx.at[0], z_rx.at[0], PEAK, z_peers)
    gather(0, 2)
    send_one(gall.at[0], gall.at[NX], RELAY, partner)
    powers(expo, TEACHER, False)
    wait_all(z_rx.at[0], recv.at[PEAK])
    joint_peak = jnp.maximum(jnp.max(z_rx[0], axis=0), local_peak)
    factor = live * jnp.exp2((local_peak - joint_peak) * TEACHER)
    t_b[...] = to_rows(factor)

    for sweep in range(SWEEPS):
        base = BASE + 5 * sweep

        def column_block(b, c):
            for s in range(TILES):
                col = expo[b, :, s * 128:(s + 1) * 128] * t_b[...]
                col_tx[pl.ds(b * TILES + s, 1), :] = jnp.sum(col, axis=0, keepdims=True)
            return c

        lax.fori_loop(0, BLOCKS, column_block, 0)
        half = BLOCKS * TILES // 2
        mine = pl.ds(pl.multiple_of(cc * half, half), half)
        other = pl.ds(pl.multiple_of((1 - cc) * half, half), half)
        push(col_tx.at[other], core_rx.at[sweep], base, [partner])
        wait_all(core_rx.at[sweep], recv.at[base])
        x_sum = col_tx[mine, :] + core_rx[sweep, 0]
        x_tx[sweep] = x_sum
        push(x_tx.at[sweep], x_rx.at[sweep], base + 1, x_peers)
        if sweep == 0:
            student_peak = logits(sf_ref, soft, False)
        if sweep == 2:
            lax.fori_loop(0, NX, shared_tables, 0)
        wait_all(x_rx.at[sweep], recv.at[base + 1])
        y_sum = x_sum + jnp.sum(x_rx[sweep], axis=0)
        y_tx[sweep] = y_sum
        push(y_tx.at[sweep], y_rx.at[sweep], base + 2, y_peers)
        if sweep == 0:
            gather(2, 6)
        if sweep == 1:
            gather(6, 8)
        if sweep == 0:
            acc[...] = jnp.zeros(acc.shape, jnp.float32)
            powers(soft, STUDENT, True)
            student_total = row_sum()
            s_tx[0:1] = student_peak
            s_tx[1:2] = student_total
            push(s_tx, s_rx, TOTALS, z_peers)
        if sweep == 2:
            wait_all(gall.at[pl.ds(NX, NX)], recv.at[RELAY])
            lax.fori_loop(NX, NX + 3, shared_tables, 0)
        wait_all(y_rx.at[sweep], recv.at[base + 2])
        p_half = 1.0 / (y_sum + jnp.sum(y_rx[sweep], axis=0))
        p_ref[sweep, mine, :] = p_half
        send_one(p_ref.at[sweep, mine], p_ref.at[sweep, mine], base + 3, partner)
        wait_all(p_ref.at[sweep, other], recv.at[base + 3])

        acc[...] = jnp.zeros(acc.shape, jnp.float32)

        def row_block(b, c):
            part = acc[...]
            for s in range(TILES):
                part += expo[b, :, s * 128:(s + 1) * 128] * p_ref[sweep, pl.ds(b * TILES + s, 1), :]
            acc[...] = part
            return c

        lax.fori_loop(0, BLOCKS, row_block, 0)
        local_row = row_sum() * factor
        z_tx[1 + sweep] = local_row
        push(z_tx.at[1 + sweep], z_rx.at[1 + sweep], base + 4, z_peers)
        if sweep == 0:
            wt[...] = jnp.transpose(w[mine_g])
            wait_all(s_rx, recv.at[TOTALS])
            top = jnp.maximum(jnp.max(s_rx[:, 0:1], axis=0), student_peak)
            total = student_total * jnp.exp2((student_peak - top) * STUDENT)
            for k in range(NZ - 1):
                total += s_rx[k, 1:2] * jnp.exp2((s_rx[k, 0:1] - top) * STUDENT)
            share = live * jnp.exp2((student_peak - top) * STUDENT) / total
            g_b[...] = to_rows(share)
            scal[0, 0:1] = local_peak
            scal[0, 1:2] = student_peak
            scal[0, 2:3] = share
            for n in range(1, BLOCKS):
                send_one(scal.at[0], scal.at[n], SCALARS, row_peers[n - 1])
        if sweep == 1:
            wait_all(scal.at[pl.ds(1, BLOCKS - 1)], recv.at[SCALARS])
            wait_all(gall.at[pl.ds(1, NX - 1)], recv.at[FEATS])
            for n in range(1, NX):
                send_one(gall.at[n], gall.at[NX + n], RELAY, partner)
        if sweep == SWEEPS - 1:
            lax.fori_loop(NX + 3, BLOCKS, shared_tables, 0)
            for s in range(TILES):
                pcol[s * 128:(s + 1) * 128, :] = to_rows(
                    p_ref[sweep, pl.ds(mine_g * TILES + s, 1), :], 128)
        wait_all(z_rx.at[1 + sweep], recv.at[base + 4])
        row = local_row + jnp.sum(z_rx[1 + sweep], axis=0)
        scale = factor / (row + (1.0 - live))
        if sweep == SWEEPS - 1:
            tall[0] = scale
            for n in range(1, BLOCKS):
                send_one(tall.at[0], tall.at[n], TOKENS, row_peers[n - 1])
        t_b[...] = to_rows(scale)
        wait_all(core_rx.at[sweep], send.at[base])
        wait_all(x_rx.at[sweep], send.at[base + 1])
        wait_all(y_rx.at[sweep], send.at[base + 2])
        wait_all(p_ref.at[sweep, other], send.at[base + 3])
        wait_all(z_rx.at[1 + sweep], send.at[base + 4])

    fpt[...] = jnp.zeros(fpt.shape, jnp.float32)

    def own_block(b, c):
        for s in range(TILES):
            lanes = slice(s * 128, (s + 1) * 128)
            target = expo[b, :, lanes] * t_b[...] * p_ref[SWEEPS - 1, pl.ds(b * TILES + s, 1), :]
            tgt[:, pl.ds(pl.multiple_of(b * WIDE + s * 128, 128), 128)] = target.astype(jnp.bfloat16)
            delta_a[:, lanes] = (soft[b, :, lanes] * g_b[...] - target).astype(jnp.bfloat16)
        fpt[...] += lax.dot_general(
            w[b], delta_a[...], NT, preferred_element_type=jnp.float32
        ).reshape(fpt.shape)
        return c

    def shared_part(q, c):
        rows = pl.ds(pl.multiple_of(q * 256, 256), 256)
        for n in range(BLOCKS):
            for h in range(2):
                lanes = slice(h * 128, (h + 1) * 128)
                target = eb[n, rows, lanes] * pcol[rows, :] * tall[n, :, lanes]
                dcat[:, n * ROWS + h * 128:n * ROWS + (h + 1) * 128] = (
                    qb[n, rows, lanes] - target).astype(jnp.bfloat16)
        grad = lax.dot_general(sft[...], dcat[...], NT, preferred_element_type=jnp.float32)
        for x in range(NX):
            for y in range(NY):
                top = (x * NY + y) * 16
                wp_tx[q, y, x * 16:(x + 1) * 16, :] = grad[top:top + 16]
        for k in range(1, NY):
            send_one(wp_tx.at[q, lax.rem(cy + k, NY)], rs_rx.at[q, k - 1], RS + q, y_peers[k - 1])
        return c

    lax.fori_loop(0, BLOCKS // 2, own_block, 0)
    wait_all(tall.at[pl.ds(1, BLOCKS - 1)], recv.at[TOKENS])
    lax.fori_loop(0, PARTS, shared_part, 0)
    lax.fori_loop(BLOCKS // 2, BLOCKS, own_block, 0)
    for k in range(1, NZ):
        send_one(fpt.at[z_place[k - 1]], f_rx.at[k - 1], FEATURE, z_peers[k - 1])

    def collect(q, c):
        wait_all(rs_rx.at[q], recv.at[RS + q])
        grad = wp_tx[q, cy] + jnp.sum(rs_rx[q], axis=0)
        a_tx[q] = grad.reshape(BLOCKS, 8, 256)
        for n in range(1, BLOCKS):
            x, core = row_place(n)
            send_one(a_tx.at[q, x * NC + core], a_rx.at[q, n - 1], SPREAD, row_peers[n - 1])
        return c

    lax.fori_loop(0, PARTS, collect, 0)
    wait_all(f_rx, recv.at[FEATURE])
    feature_ref[...] = fpt[z] + jnp.sum(f_rx[...], axis=0)
    wait_all(a_rx, recv.at[SPREAD])
    for q in range(PARTS):
        for n in range(BLOCKS):
            span = pl.ds(pl.multiple_of(row_source(n) * WIDE + q * 256, 256), 256)
            weight_ref[:, span] = a_rx[q, n - 1] if n else a_tx[q, mine_g]

    wait_all(z_rx.at[0], send.at[PEAK])
    wait_all(s_rx, send.at[TOTALS])
    wait_all(gall.at[pl.ds(1, NX - 1)], send.at[FEATS])
    wait_all(gall.at[pl.ds(NX, NX)], send.at[RELAY])
    wait_all(scal.at[pl.ds(1, BLOCKS - 1)], send.at[SCALARS])
    wait_all(tall.at[pl.ds(1, BLOCKS - 1)], send.at[TOKENS])
    wait_all(f_rx, send.at[FEATURE])
    wait_all(a_rx, send.at[SPREAD])
    for q in range(PARTS):
        wait_all(rs_rx.at[q], send.at[RS + q])


def write_out(*refs):
    sems = refs[6]
    copies = [pltpu.make_async_copy(refs[i], refs[3 + i], sems.at[i]) for i in range(3)]
    for copy in copies:
        copy.start()
    for copy in copies:
        copy.wait()


def on_device(teacher_feats, student_feats, proto_weight, token_mask):
    d, protos = proto_weight.shape
    f32, bf16 = jnp.float32, jnp.bfloat16
    vec = BLOCKS * TILES
    groups = RS + PARTS
    table = pltpu.VMEM((BLOCKS, ROWS, WIDE), f32)
    shared = pltpu.VMEM((BLOCKS, WIDE, ROWS), f32)
    rows = pltpu.VMEM((ROWS, 128), f32)
    vmem = pl.BlockSpec(memory_space=pltpu.VMEM)
    hbm = pl.BlockSpec(memory_space=pl.ANY)
    results = pl.pallas_call(
        kernel,
        out_shape=(
            pltpu.VMEM((ROWS, protos), bf16),
            pltpu.VMEM((d // (NX * NY * NC), protos), f32),
            pltpu.VMEM((d // NZ, ROWS), f32),
        ),
        in_specs=[vmem, vmem, vmem, hbm],
        out_specs=(vmem, vmem, vmem),
        scratch_shapes=[
            pltpu.VMEM((BLOCKS, d, WIDE), bf16),
            table, table, rows, rows, rows, rows,
            pltpu.VMEM((ROWS, WIDE), bf16),
            pltpu.VMEM((NZ, d // NZ, ROWS), f32),
            pltpu.VMEM((NZ - 1, d // NZ, ROWS), f32),
            pltpu.VMEM((WIDE, d), bf16),
            shared, shared,
            pltpu.VMEM((BLOCKS, 2, d, ROWS), f32),
            pltpu.VMEM((d, BLOCKS * ROWS), bf16),
            pltpu.VMEM((256, BLOCKS * ROWS), bf16),
            pltpu.VMEM((WIDE, 128), f32),
            pltpu.VMEM((BLOCKS, 3, ROWS), f32),
            pltpu.VMEM((BLOCKS, 1, ROWS), f32),
            pltpu.VMEM((PARTS, NY, d // NY, 256), f32),
            pltpu.VMEM((PARTS, NY - 1, d // NY, 256), f32),
            pltpu.VMEM((PARTS, BLOCKS, 8, 256), f32),
            pltpu.VMEM((PARTS, BLOCKS - 1, 8, 256), f32),
            pltpu.VMEM((vec, 128), f32),
            pltpu.VMEM((SWEEPS, 1, vec // 2, 128), f32),
            pltpu.VMEM((SWEEPS, vec // 2, 128), f32),
            pltpu.VMEM((SWEEPS, NX - 1, vec // 2, 128), f32),
            pltpu.VMEM((SWEEPS, vec // 2, 128), f32),
            pltpu.VMEM((SWEEPS, NY - 1, vec // 2, 128), f32),
            pltpu.VMEM((SWEEPS, vec, 128), f32),
            pltpu.VMEM((SWEEPS + 1, 1, ROWS), f32),
            pltpu.VMEM((SWEEPS + 1, NZ - 1, 1, ROWS), f32),
            pltpu.VMEM((2, ROWS), f32),
            pltpu.VMEM((NZ - 1, 2, ROWS), f32),
            pltpu.SemaphoreType.DMA((BLOCKS,)),
            pltpu.SemaphoreType.DMA((groups,)),
            pltpu.SemaphoreType.DMA((groups,)),
        ],
        compiler_params=pltpu.CompilerParams(
            collective_id=0, has_side_effects=True, vmem_limit_bytes=54 * 2**20
        ),
        name="sinkhorn",
    )(teacher_feats, student_feats, token_mask.reshape(1, -1), proto_weight)
    targets, weight_grad, feature_grad = pl.pallas_call(
        write_out,
        out_shape=tuple(jax.ShapeDtypeStruct(r.shape, r.dtype) for r in results),
        in_specs=[hbm] * 3,
        out_specs=(hbm, hbm, hbm),
        scratch_shapes=[pltpu.SemaphoreType.DMA((3,))],
        compiler_params=pltpu.CompilerParams(vmem_limit_bytes=2**20),
        name="write_out",
    )(*results)
    return targets, weight_grad, feature_grad.T


def solution(mesh):
    placed = (P("dp", None), P("dp", None), P(None, "proto"), P("dp"))
    return jax.shard_map(
        on_device,
        mesh=mesh,
        in_specs=placed,
        out_specs=(P("dp", "proto"), P("dp", "proto"), P("dp", "proto")),
        check_vma=False,
    )
```

```python
import math

import jax
import jax.numpy as jnp
from jax import lax
from jax.experimental import pallas as pl
from jax.experimental.pallas import tpu as pltpu
from jax.sharding import PartitionSpec as P

SWEEPS = 3
TEACHER = math.log2(math.e) / 0.07
STUDENT = math.log2(math.e) / 0.1
MESH = pl.DeviceIdType.MESH
NX, NY, NC, NZ = 4, 4, 2, 8
ROWS = 256
WIDE = 1024
BLOCKS = 8
HALF = BLOCKS // 2
TILES = WIDE // 128
PARTS = WIDE // 256
LINE = HALF * TILES // 2
NT = (((1,), (1,)), ((), ()))
ZC = NZ * NC - 1
FIXED = 11
PT, PS, PM, TOTALS, FEATS, RELAY, SCALARS, TOKENS, FEATURE, SPREAD, PHALF = range(FIXED)
ZS = FIXED
XS = ZS + 2 * (SWEEPS + 1)
YS = XS + 2 * SWEEPS
RS = YS + 2 * SWEEPS
GROUPS = RS + PARTS


def wait_all(ref, sem):
    pltpu.make_async_copy(ref, ref, sem).wait()


def to_rows(lanes, width=ROWS):
    return jnp.transpose(jnp.broadcast_to(lanes, (128, width)))


def kernel(
    tf_ref, sf_ref, mask_ref, w_hbm,
    tgt, weight_ref, feature_ref,
    w, expo, rest, soft, peak_b, acc, t_b, r_b, g_b, delta_a, fpt, f_rx,
    wt, eb, qb, gall, sft, dcat, pcol, scal, tall, wp_tx, rs_rx, a_tx, a_rx,
    live_ref, col, x_tx, x_rx, y_tx, y_rx, p_ref,
    z_tx, z_rx, s_tx, s_rx,
    w_sem, send, recv,
):
    dp = lax.axis_index("dp")
    z = lax.axis_index("proto")
    cx, cy, cc = dp // (NY * NC), lax.rem(dp // NC, NY), lax.rem(dp, NC)

    def at(x, y, c):
        return {"dp": (x * NY + y) * NC + c}

    def row_place(n):
        x = lax.rem(cx + n % NX, NX)
        return x, (cc if n < NX else 1 - cc)

    def row_source(n):
        x = lax.rem(cx + NX - n % NX, NX)
        return x, (cc if n < NX else 1 - cc)

    partner = at(cx, cy, 1 - cc)
    row_peers = [at(row_place(n)[0], cy, row_place(n)[1]) for n in range(1, BLOCKS)]
    x_peers = row_peers[: NX - 1]
    y_peers = [at(cx, lax.rem(cy + k, NY), cc) for k in range(1, NY)]
    z_place = [lax.rem(z + k, NZ) for k in range(1, NZ)]
    z_peers = [{"proto": place} for place in z_place]
    zc_peers = z_peers + [partner] + [
        {"dp": dp + 1 - 2 * cc, "proto": place} for place in z_place]

    barrier = pltpu.get_barrier_semaphore()
    peers = row_peers + y_peers + z_peers + zc_peers[NZ:]
    for peer in peers:
        pl.semaphore_signal(barrier, inc=1, device_id=peer, device_id_type=MESH)

    def column(v):
        return pl.multiple_of(lax.rem(cc * HALF + v, BLOCKS) * WIDE, WIDE)

    def load(v):
        return pltpu.make_async_copy(w_hbm.at[:, pl.ds(column(v), WIDE)], w.at[v], w_sem.at[v])

    def start_load(v, c):
        load(v).start()
        return c

    lax.fori_loop(0, BLOCKS, start_load, 0)

    def wait_load(v, c):
        load(v).wait()
        return c

    def send_one(src, dst, group, device):
        pltpu.make_async_remote_copy(
            src_ref=src, dst_ref=dst, send_sem=send.at[group], recv_sem=recv.at[group],
            device_id=device, device_id_type=MESH,
        ).start()

    def push(src, dst, group, devices):
        for k, device in enumerate(devices):
            send_one(src, dst.at[k], group, device)

    def push_z(slot, tc):
        for n in (4, 12, 3, 5, 11, 13, 2, 6, 10, 14, 1, 7, 9, 15, 8):
            send_one(z_tx.at[slot, tc], z_rx.at[slot, tc, n - 1], ZS + 2 * slot + tc,
                     zc_peers[n - 1])

    def wait_z(slot, tc):
        wait_all(z_rx.at[slot, tc], recv.at[ZS + 2 * slot + tc])

    def gather(first, last):
        def piece(q, c):
            for n in range(1, NX):
                at_q = (q // 4, pl.ds(pl.multiple_of(q % 4 * 64, 64), 64))
                send_one(gall.at[(0,) + at_q], gall.at[(n,) + at_q], FEATS, x_peers[n - 1])
            return c

        lax.fori_loop(first, last, piece, 0)

    def logits(feats, table, blocks, first):
        acc[0] = jnp.full(acc.shape[1:], -jnp.inf, jnp.float32)

        def block(v, c):
            if first:
                load(v).wait()
            for s in range(PARTS):
                part = jnp.dot(
                    feats[...], w[v, :, s * 256:(s + 1) * 256],
                    preferred_element_type=jnp.float32,
                )
                table[v, :, s * 256:(s + 1) * 256] = part
                acc[0] = jnp.maximum(acc[0], jnp.maximum(part[:, :128], part[:, 128:]))
            return c

        lax.fori_loop(0, blocks, block, 0)
        peak_b[...] = jnp.broadcast_to(jnp.max(acc[0], axis=1, keepdims=True), peak_b.shape)
        return jnp.max(jnp.transpose(acc[0]), axis=0, keepdims=True)

    def powers(table, scale, blocks, total):
        def block(v, c):
            for s in range(TILES):
                at_s = (v, slice(None), slice(s * 128, (s + 1) * 128))
                value = jnp.exp2((table[at_s] - peak_b[...]) * scale)
                table[at_s] = value
                if total:
                    acc[0] += value
            return c

        lax.fori_loop(0, blocks, block, 0)

    def row_sum(tc):
        return jnp.sum(jnp.transpose(acc[tc]), axis=0, keepdims=True)

    def rest_table():
        def block(v, c):
            for s in range(PARTS):
                part = jnp.dot(
                    tf_ref[...], w[HALF + v, :, s * 256:(s + 1) * 256],
                    preferred_element_type=jnp.float32,
                )
                for h in range(2):
                    rest[v, :, s * 256 + h * 128:s * 256 + (h + 1) * 128] = jnp.exp2(
                        (part[:, h * 128:(h + 1) * 128] - r_b[...]) * TEACHER)
            return c

        lax.fori_loop(0, HALF, block, 0)

    def shared_tables(n, c):
        feats_t = gall[n, 0].astype(jnp.bfloat16)
        feats_s = gall[n, 1].astype(jnp.bfloat16)
        sft[:, pl.ds(pl.multiple_of(n * ROWS, ROWS), ROWS)] = feats_s
        for q in range(PARTS):
            rows = slice(q * 256, (q + 1) * 256)
            dot = jnp.dot(wt[rows, :], feats_t, preferred_element_type=jnp.float32)
            eb[n, rows, :] = jnp.exp2((dot - scal[n, 0:1]) * TEACHER)
            dot = jnp.dot(wt[rows, :], feats_s, preferred_element_type=jnp.float32)
            qb[n, rows, :] = jnp.exp2((dot - scal[n, 1:2]) * STUDENT) * scal[n, 2:3]
        return c

    live = mask_ref[...].astype(jnp.float32)
    live_ref[cc] = live
    own = expo.at[cc]
    others = expo.at[1 - cc]
    z_tx[0, cc] = logits(tf_ref, own, HALF, True)
    gall[0, 0] = jnp.transpose(tf_ref[...].astype(jnp.float32))
    pl.semaphore_wait(barrier, len(peers))
    send_one(gall.at[0, 0], gall.at[NX, 0], PT, partner)
    send_one(live_ref.at[cc], live_ref.at[cc], PM, partner)
    push_z(0, cc)
    powers(own, TEACHER, HALF, False)
    wait_all(gall.at[NX, 0], recv.at[PT])
    delta_a[:, :ROWS] = jnp.transpose(gall[NX, 0].astype(jnp.bfloat16))
    z_tx[0, 1 - cc] = logits(delta_a.at[:, pl.ds(0, ROWS)], others, HALF, False)
    push_z(0, 1 - cc)
    gall[0, 1] = jnp.transpose(sf_ref[...].astype(jnp.float32))
    send_one(gall.at[0, 1], gall.at[NX, 1], PS, partner)
    gather(0, 2)
    powers(others, TEACHER, HALF, False)
    wait_all(live_ref.at[1 - cc], recv.at[PM])

    peaks, factors = [], []
    half_rows = HALF * TILES
    for sweep in range(SWEEPS):
        for tc in range(NC):
            wait_z(sweep, tc)
            if sweep == 0:
                peak = jnp.maximum(jnp.max(z_rx[0, tc], axis=0), z_tx[0, tc])
                peaks.append(peak)
                factors.append(live_ref[tc] * jnp.exp2((z_tx[0, tc] - peak) * TEACHER))
                scale = factors[tc]
            else:
                row = z_tx[sweep, tc] + jnp.sum(z_rx[sweep, tc], axis=0)
                scale = factors[tc] / (row + (1.0 - live_ref[tc]))
            t_b[...] = to_rows(scale)
            for part in range(2):
                def column_block(v, c):
                    for s in range(TILES):
                        r = (v - part * (HALF // 2)) * TILES + s
                        total = jnp.sum(
                            expo[tc, v, :, s * 128:(s + 1) * 128] * t_b[...],
                            axis=0, keepdims=True)
                        if tc:
                            x_tx[sweep, part, pl.ds(r, 1), :] = (
                                col[part, pl.ds(r, 1), :] + total)
                        else:
                            col[part, pl.ds(r, 1), :] = total
                    return c

                lax.fori_loop(part * (HALF // 2), (part + 1) * (HALF // 2), column_block, 0)
                if tc:
                    group = XS + 2 * sweep + part
                    push(x_tx.at[sweep, part], x_rx.at[sweep, part], group, x_peers)

        if sweep == 0:
            lax.fori_loop(HALF, BLOCKS, wait_load, 0)
            student_peak = logits(sf_ref, soft, BLOCKS, False)
        if sweep == 1:
            r_b[...] = to_rows(jnp.where(cc == 0, peaks[0], peaks[1]))
            rest_table()
        if sweep == 2:
            wait_all(gall.at[pl.ds(1, NX - 1)], recv.at[FEATS])
            for n in range(1, NX):
                send_one(gall.at[n], gall.at[NX + n], RELAY, partner)
            lax.fori_loop(0, 3, shared_tables, 0)
        for part in range(2):
            wait_all(x_rx.at[sweep, part], recv.at[XS + 2 * sweep + part])
            y_tx[sweep, part] = x_tx[sweep, part] + jnp.sum(x_rx[sweep, part], axis=0)
            push(y_tx.at[sweep, part], y_rx.at[sweep, part], YS + 2 * sweep + part, y_peers)
        if sweep == 0:
            gather(2, 5)
            acc[0] = jnp.zeros(acc.shape[1:], jnp.float32)
            powers(soft, STUDENT, BLOCKS, True)
            student_total = row_sum(0)
            s_tx[0:1] = student_peak
            s_tx[1:2] = student_total
            push(s_tx, s_rx, TOTALS, z_peers)
        if sweep == 1:
            gather(5, 8)
        if sweep == 2:
            lax.fori_loop(3, 5, shared_tables, 0)
        acc[...] = jnp.zeros(acc.shape, jnp.float32)
        for part in range(2):
            wait_all(y_rx.at[sweep, part], recv.at[YS + 2 * sweep + part])
            p_ref[part * LINE:(part + 1) * LINE] = 1.0 / (
                y_tx[sweep, part] + jnp.sum(y_rx[sweep, part], axis=0))
            if part and sweep == SWEEPS - 1:
                send_one(p_ref.at[pl.ds(0, half_rows)], p_ref.at[pl.ds(half_rows, half_rows)],
                         PHALF, partner)
            for tc in range(NC):
                def row_block(v, c):
                    total = acc[tc]
                    for s in range(TILES):
                        total += (expo[tc, v, :, s * 128:(s + 1) * 128]
                                  * p_ref[pl.ds(v * TILES + s, 1), :])
                    acc[tc] = total
                    return c

                lax.fori_loop(part * (HALF // 2), (part + 1) * (HALF // 2), row_block, 0)
                if part:
                    z_tx[sweep + 1, tc] = row_sum(tc) * factors[tc]
                    push_z(sweep + 1, tc)
        if sweep == 0:
            wt[...] = jnp.transpose(w[cx])
            wait_all(s_rx, recv.at[TOTALS])
            top = jnp.maximum(jnp.max(s_rx[:, 0:1], axis=0), student_peak)
            total = student_total * jnp.exp2((student_peak - top) * STUDENT)
            for k in range(NZ - 1):
                total += s_rx[k, 1:2] * jnp.exp2((s_rx[k, 0:1] - top) * STUDENT)
            share = live * jnp.exp2((student_peak - top) * STUDENT) / total
            g_b[...] = to_rows(share)
            scal[0, 0:1] = jnp.where(cc == 0, peaks[0], peaks[1])
            scal[0, 1:2] = student_peak
            scal[0, 2:3] = share
            for n in range(1, BLOCKS):
                send_one(scal.at[0], scal.at[n], SCALARS, row_peers[n - 1])
        if sweep == 1:
            wait_all(scal.at[pl.ds(1, BLOCKS - 1)], recv.at[SCALARS])
            wait_all(gall.at[NX, 1], recv.at[PS])
        if sweep == SWEEPS - 1:
            wait_all(gall.at[pl.ds(NX + 1, NX - 1)], recv.at[RELAY])
            lax.fori_loop(5, BLOCKS, shared_tables, 0)
            for s in range(TILES):
                pcol[s * 128:(s + 1) * 128, :] = to_rows(
                    p_ref[pl.ds(cx * TILES + s, 1), :], 128)

    wait_z(SWEEPS, cc)
    row = z_tx[SWEEPS, cc] + jnp.sum(z_rx[SWEEPS, cc], axis=0)
    scale = 1.0 / (row + (1.0 - live))
    tall[0] = scale * live
    for n in range(1, BLOCKS):
        send_one(tall.at[0], tall.at[n], TOKENS, row_peers[n - 1])
    wait_z(SWEEPS, 1 - cc)
    t_b[...] = to_rows(scale * jnp.where(cc == 0, factors[0], factors[1]))
    r_b[...] = to_rows(scale * live)
    fpt[...] = jnp.zeros(fpt.shape, jnp.float32)

    def own_block(table, factor, v):
        base = column(v)
        for s in range(TILES):
            lanes = slice(s * 128, (s + 1) * 128)
            target = table[:, lanes] * factor[...] * p_ref[pl.ds(v * TILES + s, 1), :]
            tgt[:, pl.ds(pl.multiple_of(base + s * 128, 128), 128)] = target.astype(jnp.bfloat16)
            delta_a[:, lanes] = (soft[v, :, lanes] * g_b[...] - target).astype(jnp.bfloat16)
        fpt[...] += lax.dot_general(
            w[v], delta_a[...], NT, preferred_element_type=jnp.float32
        ).reshape(fpt.shape)

    def first_half(v, c):
        own_block(own.at[v], t_b, v)
        return c

    def second_half(v, c):
        own_block(rest.at[v], r_b, HALF + v)
        return c

    def shared_part(q, c):
        rows = pl.ds(pl.multiple_of(q * 256, 256), 256)
        for n in range(BLOCKS):
            for h in range(2):
                lanes = slice(h * 128, (h + 1) * 128)
                target = eb[n, rows, lanes] * pcol[rows, :] * tall[n, :, lanes]
                dcat[:, n * ROWS + h * 128:n * ROWS + (h + 1) * 128] = (
                    qb[n, rows, lanes] - target).astype(jnp.bfloat16)
        grad = lax.dot_general(sft[...], dcat[...], NT, preferred_element_type=jnp.float32)
        for x in range(NX):
            for y in range(NY):
                top = (x * NY + y) * 16
                wp_tx[q, y, x * 16:(x + 1) * 16, :] = grad[top:top + 16]
        for k in range(1, NY):
            send_one(wp_tx.at[q, lax.rem(cy + k, NY)], rs_rx.at[q, k - 1], RS + q, y_peers[k - 1])
        return c

    lax.fori_loop(0, HALF, first_half, 0)
    wait_all(tall.at[pl.ds(1, BLOCKS - 1)], recv.at[TOKENS])
    lax.fori_loop(0, PARTS, shared_part, 0)
    wait_all(p_ref.at[pl.ds(half_rows, half_rows)], recv.at[PHALF])
    lax.fori_loop(0, HALF, second_half, 0)
    for k in range(1, NZ):
        send_one(fpt.at[z_place[k - 1]], f_rx.at[k - 1], FEATURE, z_peers[k - 1])

    def collect(q, c):
        wait_all(rs_rx.at[q], recv.at[RS + q])
        grad = wp_tx[q, cy] + jnp.sum(rs_rx[q], axis=0)
        a_tx[q] = grad.reshape(BLOCKS, 8, 256)
        for n in range(1, BLOCKS):
            x, core = row_place(n)
            send_one(a_tx.at[q, x * NC + core], a_rx.at[q, n - 1], SPREAD, row_peers[n - 1])
        return c

    lax.fori_loop(0, PARTS, collect, 0)
    wait_all(f_rx, recv.at[FEATURE])
    feature_ref[...] = fpt[z] + jnp.sum(f_rx[...], axis=0)
    wait_all(a_rx, recv.at[SPREAD])
    for q in range(PARTS):
        for n in range(BLOCKS):
            x, core = row_source(n)
            span = pl.ds(pl.multiple_of((core * HALF + x) * WIDE + q * 256, 256), 256)
            weight_ref[:, span] = a_rx[q, n - 1] if n else a_tx[q, cx * NC + cc]

    wait_all(gall.at[NX, 0], send.at[PT])
    wait_all(gall.at[NX, 1], send.at[PS])
    wait_all(live_ref.at[1 - cc], send.at[PM])
    wait_all(s_rx, send.at[TOTALS])
    wait_all(gall.at[pl.ds(1, NX - 1)], send.at[FEATS])
    wait_all(gall.at[pl.ds(NX + 1, NX - 1)], send.at[RELAY])
    wait_all(scal.at[pl.ds(1, BLOCKS - 1)], send.at[SCALARS])
    wait_all(tall.at[pl.ds(1, BLOCKS - 1)], send.at[TOKENS])
    wait_all(f_rx, send.at[FEATURE])
    wait_all(a_rx, send.at[SPREAD])
    wait_all(p_ref.at[pl.ds(half_rows, half_rows)], send.at[PHALF])
    for slot in range(SWEEPS + 1):
        for tc in range(NC):
            wait_all(z_rx.at[slot, tc], send.at[ZS + 2 * slot + tc])
    for sweep in range(SWEEPS):
        for part in range(2):
            wait_all(x_rx.at[sweep, part], send.at[XS + 2 * sweep + part])
            wait_all(y_rx.at[sweep, part], send.at[YS + 2 * sweep + part])
    for q in range(PARTS):
        wait_all(rs_rx.at[q], send.at[RS + q])


def write_out(*refs):
    sems = refs[6]
    copies = [pltpu.make_async_copy(refs[i], refs[3 + i], sems.at[i]) for i in range(3)]
    for copy in copies:
        copy.start()
    for copy in copies:
        copy.wait()


def on_device(teacher_feats, student_feats, proto_weight, token_mask):
    d, protos = proto_weight.shape
    f32, bf16 = jnp.float32, jnp.bfloat16
    shared = pltpu.VMEM((BLOCKS, WIDE, ROWS), f32)
    rows = pltpu.VMEM((ROWS, 128), f32)
    vmem = pl.BlockSpec(memory_space=pltpu.VMEM)
    hbm = pl.BlockSpec(memory_space=pl.ANY)
    results = pl.pallas_call(
        kernel,
        out_shape=(
            pltpu.VMEM((ROWS, protos), bf16),
            pltpu.VMEM((d // (NX * NY * NC), protos), f32),
            pltpu.VMEM((d // NZ, ROWS), f32),
        ),
        in_specs=[vmem, vmem, vmem, hbm],
        out_specs=(vmem, vmem, vmem),
        scratch_shapes=[
            pltpu.VMEM((BLOCKS, d, WIDE), bf16),
            pltpu.VMEM((NC, HALF, ROWS, WIDE), f32),
            pltpu.VMEM((HALF, ROWS, WIDE), f32),
            pltpu.VMEM((BLOCKS, ROWS, WIDE), f32),
            rows,
            pltpu.VMEM((NC, ROWS, 128), f32),
            rows, rows, rows,
            pltpu.VMEM((ROWS, WIDE), bf16),
            pltpu.VMEM((NZ, d // NZ, ROWS), f32),
            pltpu.VMEM((NZ - 1, d // NZ, ROWS), f32),
            pltpu.VMEM((WIDE, d), bf16),
            shared, shared,
            pltpu.VMEM((BLOCKS, 2, d, ROWS), f32),
            pltpu.VMEM((d, BLOCKS * ROWS), bf16),
            pltpu.VMEM((256, BLOCKS * ROWS), bf16),
            pltpu.VMEM((WIDE, 128), f32),
            pltpu.VMEM((BLOCKS, 3, ROWS), f32),
            pltpu.VMEM((BLOCKS, 1, ROWS), f32),
            pltpu.VMEM((PARTS, NY, d // NY, 256), f32),
            pltpu.VMEM((PARTS, NY - 1, d // NY, 256), f32),
            pltpu.VMEM((PARTS, BLOCKS, 8, 256), f32),
            pltpu.VMEM((PARTS, BLOCKS - 1, 8, 256), f32),
            pltpu.VMEM((NC, 1, ROWS), f32),
            pltpu.VMEM((2, LINE, 128), f32),
            pltpu.VMEM((SWEEPS, 2, LINE, 128), f32),
            pltpu.VMEM((SWEEPS, 2, NX - 1, LINE, 128), f32),
            pltpu.VMEM((SWEEPS, 2, LINE, 128), f32),
            pltpu.VMEM((SWEEPS, 2, NY - 1, LINE, 128), f32),
            pltpu.VMEM((BLOCKS * TILES, 128), f32),
            pltpu.VMEM((SWEEPS + 1, NC, 1, ROWS), f32),
            pltpu.VMEM((SWEEPS + 1, NC, ZC, 1, ROWS), f32),
            pltpu.VMEM((2, ROWS), f32),
            pltpu.VMEM((NZ - 1, 2, ROWS), f32),
            pltpu.SemaphoreType.DMA((BLOCKS,)),
            pltpu.SemaphoreType.DMA((GROUPS,)),
            pltpu.SemaphoreType.DMA((GROUPS,)),
        ],
        compiler_params=pltpu.CompilerParams(
            collective_id=0, has_side_effects=True, vmem_limit_bytes=58 * 2**20
        ),
        name="sinkhorn",
    )(teacher_feats, student_feats, token_mask.reshape(1, -1), proto_weight)
    targets, weight_grad, feature_grad = pl.pallas_call(
        write_out,
        out_shape=tuple(jax.ShapeDtypeStruct(r.shape, r.dtype) for r in results),
        in_specs=[hbm] * 3,
        out_specs=(hbm, hbm, hbm),
        scratch_shapes=[pltpu.SemaphoreType.DMA((3,))],
        compiler_params=pltpu.CompilerParams(vmem_limit_bytes=2**20),
        name="write_out",
    )(*results)
    return targets, weight_grad, feature_grad.T


def solution(mesh):
    placed = (P("dp", None), P("dp", None), P(None, "proto"), P("dp"))
    return jax.shard_map(
        on_device,
        mesh=mesh,
        in_specs=placed,
        out_specs=(P("dp", "proto"), P("dp", "proto"), P("dp", "proto")),
        check_vma=False,
    )
```

```python
import math

import jax
import jax.numpy as jnp
from jax import lax
from jax.experimental import pallas as pl
from jax.experimental.pallas import tpu as pltpu
from jax.sharding import PartitionSpec as P

SWEEPS = 3
TEACHER = math.log2(math.e) / 0.07
STUDENT = math.log2(math.e) / 0.1
MESH = pl.DeviceIdType.MESH
NX, NY, NC, NZ = 4, 4, 2, 8
ROWS = 256
WIDE = 1024
BLOCKS = 8
HALF = BLOCKS // 2
TILES = WIDE // 128
PARTS = WIDE // 256
THIN = WIDE // 2
SUBS = THIN // 256
SLOTS = 14
TH = ROWS // 2
LINE = HALF * TILES // 2
NT = (((1,), (1,)), ((), ()))
ZC = NZ * NC - 1
FIXED = 20
PT, PS, PM, TOTALS, SCALARS, TOKENS, PHALF, PEAK = range(8)
FEATS, RELAY, FEATURE, SPREAD = 8, 12, 16, 18
ZS = FIXED
XS = ZS + 2 * SWEEPS
YS = XS + 2 * SWEEPS
RS = YS + 2 * SWEEPS
GROUPS = RS + 2 * SUBS


def wait_all(ref, sem):
    pltpu.make_async_copy(ref, ref, sem).wait()


def to_rows(lanes, width=ROWS):
    return jnp.transpose(jnp.broadcast_to(lanes, (128, width)))


def kernel(
    tf_ref, sf_ref, mask_ref, w_hbm,
    tgt, weight_ref, feature_ref,
    w, expo, rest, soft, peak_b, acc, t_b, r_b, g_b, delta_a, fpt, f_rx,
    wt, eb, qb, gall, sft, dcat, pcol, scal, tall, wp_tx, rs_rx, a_tx, a_rx,
    live_ref, k_rx, col, x_tx, x_rx, y_tx, y_rx, p_ref,
    z_tx, z_rx, s_tx, s_rx,
    w_sem, send, recv,
):
    dp = lax.axis_index("dp")
    z = lax.axis_index("proto")
    cx, cy, cc = dp // (NY * NC), lax.rem(dp // NC, NY), lax.rem(dp, NC)

    def at(x, y, c):
        return {"dp": (x * NY + y) * NC + c}

    here = (cx, cy)

    def place(a, n):
        return lax.rem(here[a] + n % NX, NX), (cc if n < NX else 1 - cc)

    def source(a, n):
        return lax.rem(here[a] + NX - n % NX, NX), (cc if n < NX else 1 - cc)

    def peer_of(a, n):
        far, core = place(a, n)
        return at(cx, far, core) if a else at(far, cy, core)

    def slot_of(a, n):
        if a == 0 or n % NX == 0:
            return n
        return n + 7 if n < NX else n + 6

    partner = at(cx, cy, 1 - cc)
    shared_peers = [(slot_of(a, n), peer_of(a, n))
                    for a in range(2) for n in range(1, BLOCKS) if a == 0 or n != NX]
    x_peers = [peer_of(0, k) for k in range(1, NX)]
    y_peers = [peer_of(1, k) for k in range(1, NY)]
    axis_peers = (x_peers, y_peers)
    z_place = [lax.rem(z + k, NZ) for k in range(1, NZ)]
    z_peers = [{"proto": place} for place in z_place]
    zc_peers = z_peers + [partner] + [
        {"dp": dp + 1 - 2 * cc, "proto": place} for place in z_place]

    barrier = pltpu.get_barrier_semaphore()
    peers = [peer for _, peer in shared_peers] + z_peers + zc_peers[NZ:]
    for peer in peers:
        pl.semaphore_signal(barrier, inc=1, device_id=peer, device_id_type=MESH)

    def column(v):
        return pl.multiple_of(lax.rem(cc * HALF + v, BLOCKS) * WIDE, WIDE)

    def load(v):
        return pltpu.make_async_copy(w_hbm.at[:, pl.ds(column(v), WIDE)], w.at[v], w_sem.at[v])

    def start_load(v, c):
        load(v).start()
        return c

    lax.fori_loop(0, BLOCKS, start_load, 0)

    def send_one(src, dst, group, device):
        pltpu.make_async_remote_copy(
            src_ref=src, dst_ref=dst, send_sem=send.at[group], recv_sem=recv.at[group],
            device_id=device, device_id_type=MESH,
        ).start()

    def push(src, dst, group, devices):
        for k, device in enumerate(devices):
            send_one(src, dst.at[k], group, device)

    far_first = (12, 4, 11, 13, 3, 5, 10, 14, 2, 6, 9, 15, 1, 7, 8)

    def push_z(slot, tc):
        for n in far_first:
            send_one(z_tx.at[slot, tc], z_rx.at[slot, tc, n - 1], ZS + 2 * slot + tc,
                     zc_peers[n - 1])

    def wait_z(slot, tc):
        wait_all(z_rx.at[slot, tc], recv.at[ZS + 2 * slot + tc])

    def gather(a, first, last):
        for q in range(first, last):
            rows = pl.ds(q % 4 * 64, 64)
            for n in range(1, NX):
                send_one(gall.at[q // 4, 0, rows], gall.at[q // 4, slot_of(a, n), rows],
                         FEATS + 2 * a + q // 4, axis_peers[a][n - 1])

    def arrivals(a, t, core):
        return gall.at[t, pl.ds(slot_of(a, core * NX + 1), NX - 1)]

    def relay(t):
        for a in range(2):
            wait_all(arrivals(a, t, 0), recv.at[FEATS + 2 * a + t])
            send_one(arrivals(a, t, 0), arrivals(a, t, 1), RELAY + 2 * a + t, partner)

    def logits(feats, table, low, high, first):
        def block(v, c):
            if first:
                load(v).wait()
            part = jnp.dot(feats[...], w[v], preferred_element_type=jnp.float32)
            table[v - low] = part
            most = part[:, :128]
            for s in range(1, TILES):
                most = jnp.maximum(most, part[:, s * 128:(s + 1) * 128])
            acc[0] = jnp.maximum(acc[0], most)
            return c

        lax.fori_loop(low, high, block, 0)

    def no_peak():
        acc[0] = jnp.full(acc.shape[1:], -jnp.inf, jnp.float32)

    def found_peak():
        return jnp.max(jnp.transpose(acc[0]), axis=0, keepdims=True)

    def powers(table, peak, scale, blocks, total):
        def block(v, c):
            for s in range(TILES):
                at_s = (v, slice(None), slice(s * 128, (s + 1) * 128))
                value = jnp.exp2((table[at_s] - peak[...]) * scale)
                table[at_s] = value
                if total:
                    acc[0] += value
            return c

        lax.fori_loop(0, blocks, block, 0)

    def row_sum(tc):
        return jnp.sum(jnp.transpose(acc[tc]), axis=0, keepdims=True)

    def partner_table(feats, peak):
        def block(v, c):
            for s in range(PARTS):
                part = jnp.dot(
                    feats[...], w[v, :, s * 256:(s + 1) * 256],
                    preferred_element_type=jnp.float32,
                )
                for h in range(2):
                    others[v, :, s * 256 + h * 128:s * 256 + (h + 1) * 128] = jnp.exp2(
                        (part[:, h * 128:(h + 1) * 128] - peak[...]) * TEACHER)
            return c

        lax.fori_loop(0, HALF, block, 0)

    def shared_tables(t, places):
        for a in range(2):
            for n in places:
                slot = slot_of(a, n)
                feats = gall[t, slot].astype(jnp.bfloat16)
                if t:
                    sft[a, :, n * ROWS:(n + 1) * ROWS] = feats
                for q in range(SUBS):
                    rows = slice(q * 256, (q + 1) * 256)
                    dot = jnp.dot(wt[a, rows, :], feats, preferred_element_type=jnp.float32)
                    if t:
                        qb[a, n, rows, :] = jnp.exp2(
                            (dot - scal[slot, 1:2]) * STUDENT) * scal[slot, 2:3]
                    else:
                        eb[a, n, rows, :] = jnp.exp2((dot - scal[slot, 0:1]) * TEACHER)

    live = mask_ref[...].astype(jnp.float32)
    own = expo.at[cc]
    others = expo.at[1 - cc]
    gall[0, 0] = jnp.transpose(tf_ref[...].astype(jnp.float32))
    no_peak()
    logits(tf_ref, own, 0, HALF, True)
    logits(tf_ref, rest, HALF, BLOCKS, True)
    local_peak = found_peak()
    live_ref[cc, 0] = live
    live_ref[cc, 1] = local_peak
    pl.semaphore_wait(barrier, len(peers))
    for n in far_first:
        send_one(live_ref.at[cc, 1], k_rx.at[n - 1], PEAK, zc_peers[n - 1])
    send_one(gall.at[0, 0], gall.at[0, NX], PT, partner)
    send_one(live_ref.at[cc], live_ref.at[cc], PM, partner)
    gather(0, 0, 2)
    gather(1, 0, 3)
    r_b[...] = to_rows(local_peak)
    powers(own, r_b, TEACHER, HALF, False)
    wait_all(gall.at[0, NX], recv.at[PT])
    delta_a[:, :ROWS] = jnp.transpose(gall[0, NX].astype(jnp.bfloat16))
    wait_all(live_ref.at[1 - cc], recv.at[PM])
    t_b[...] = to_rows(live_ref[1 - cc, 1])
    partner_table(delta_a.at[:, pl.ds(0, ROWS)], t_b)
    gall[1, 0] = jnp.transpose(sf_ref[...].astype(jnp.float32))
    send_one(gall.at[1, 0], gall.at[1, NX], PS, partner)

    wait_all(k_rx, recv.at[PEAK])
    joint_peak = jnp.maximum(jnp.max(k_rx[:NZ - 1], axis=0), local_peak)
    own_factor = live * jnp.exp2((local_peak - joint_peak) * TEACHER)
    other_factor = live_ref[1 - cc, 0] * jnp.exp2(
        (live_ref[1 - cc, 1] - jnp.max(k_rx[NZ - 1:], axis=0)) * TEACHER)
    factors = [jnp.where(cc == tc, own_factor, other_factor) for tc in range(NC)]
    half_rows = HALF * TILES
    for sweep in range(SWEEPS):
        for tc in range(NC):
            scale = factors[tc]
            if sweep:
                wait_z(sweep - 1, tc)
                row = z_tx[sweep - 1, tc] + jnp.sum(z_rx[sweep - 1, tc], axis=0)
                scale = scale / (row + (1.0 - live_ref[tc, 0]))
            t_b[...] = to_rows(scale)
            for part in range(2):
                def column_block(v, c):
                    for s in range(TILES):
                        r = (v - part * (HALF // 2)) * TILES + s
                        total = jnp.sum(
                            expo[tc, v, :, s * 128:(s + 1) * 128] * t_b[...],
                            axis=0, keepdims=True)
                        if tc:
                            x_tx[sweep, part, pl.ds(r, 1), :] = (
                                col[part, pl.ds(r, 1), :] + total)
                        else:
                            col[part, pl.ds(r, 1), :] = total
                    return c

                lax.fori_loop(part * (HALF // 2), (part + 1) * (HALF // 2), column_block, 0)
                if tc:
                    group = XS + 2 * sweep + part
                    push(x_tx.at[sweep, part], x_rx.at[sweep, part], group, x_peers)

        if sweep == 0:
            no_peak()
            logits(sf_ref, soft, 0, BLOCKS, False)
            student_peak = found_peak()
            peak_b[...] = to_rows(student_peak)
        if sweep == 1:
            powers(rest, r_b, TEACHER, HALF, False)
        if sweep == 2:
            relay(1)
            for a in range(2):
                wait_all(arrivals(a, 0, 1), recv.at[RELAY + 2 * a])
            shared_tables(0, range(NX, BLOCKS))
        for part in range(2):
            wait_all(x_rx.at[sweep, part], recv.at[XS + 2 * sweep + part])
            y_tx[sweep, part] = x_tx[sweep, part] + jnp.sum(x_rx[sweep, part], axis=0)
            push(y_tx.at[sweep, part], y_rx.at[sweep, part], YS + 2 * sweep + part, y_peers)
        if sweep == 0:
            gather(0, 2, 5)
            acc[0] = jnp.zeros(acc.shape[1:], jnp.float32)
            powers(soft, peak_b, STUDENT, BLOCKS, True)
            student_total = row_sum(0)
            s_tx[0:1] = student_peak
            s_tx[1:2] = student_total
            push(s_tx, s_rx, TOTALS, z_peers)
        if sweep == 1:
            gather(0, 5, 8)
            relay(0)
        if sweep == 2:
            shared_tables(1, range(1, NX))
        acc[...] = jnp.zeros(acc.shape, jnp.float32)
        for part in range(2):
            wait_all(y_rx.at[sweep, part], recv.at[YS + 2 * sweep + part])
            p_ref[part * LINE:(part + 1) * LINE] = 1.0 / (
                y_tx[sweep, part] + jnp.sum(y_rx[sweep, part], axis=0))
            if part and sweep == SWEEPS - 1:
                send_one(p_ref.at[pl.ds(0, half_rows)], p_ref.at[pl.ds(half_rows, half_rows)],
                         PHALF, partner)
            for tc in range(NC):
                def row_block(v, c):
                    total = acc[tc]
                    for s in range(TILES):
                        total += (expo[tc, v, :, s * 128:(s + 1) * 128]
                                  * p_ref[pl.ds(v * TILES + s, 1), :])
                    acc[tc] = total
                    return c

                lax.fori_loop(part * (HALF // 2), (part + 1) * (HALF // 2), row_block, 0)
                if part:
                    z_tx[sweep, tc] = row_sum(tc) * factors[tc]
                    push_z(sweep, tc)
        if sweep == 0:
            gather(1, 3, 6)
            for a in range(2):
                lanes = pl.ds(pl.multiple_of(lax.rem(here[a], 2) * THIN, THIN), THIN)
                wt[a] = jnp.transpose(w[2 * a + here[a] // 2, :, lanes])
            wait_all(s_rx, recv.at[TOTALS])
            top = jnp.maximum(jnp.max(s_rx[:, 0:1], axis=0), student_peak)
            total = student_total * jnp.exp2((student_peak - top) * STUDENT)
            for k in range(NZ - 1):
                total += s_rx[k, 1:2] * jnp.exp2((s_rx[k, 0:1] - top) * STUDENT)
            share = live * jnp.exp2((student_peak - top) * STUDENT) / total
            g_b[...] = to_rows(share)
            scal[0, 0:1] = joint_peak
            scal[0, 1:2] = student_peak
            scal[0, 2:3] = share
            for slot, peer in shared_peers:
                send_one(scal.at[0], scal.at[slot], SCALARS, peer)
        if sweep == 1:
            gather(1, 6, 8)
            wait_all(scal.at[pl.ds(1, SLOTS - 1)], recv.at[SCALARS])
            wait_all(gall.at[1, NX], recv.at[PS])
            shared_tables(0, range(NX))
            shared_tables(1, (0, NX))
        if sweep == SWEEPS - 1:
            for a in range(2):
                wait_all(arrivals(a, 1, 1), recv.at[RELAY + 2 * a + 1])
            shared_tables(1, range(NX + 1, BLOCKS))
            for a in range(2):
                for s in range(TILES // 2):
                    line = a * LINE + here[a] * (TILES // 2) + s
                    pcol[a, s * 128:(s + 1) * 128, :] = to_rows(p_ref[pl.ds(line, 1), :], 128)

    scales = []
    for tc in range(NC):
        wait_z(SWEEPS - 1, tc)
        row = z_tx[SWEEPS - 1, tc] + jnp.sum(z_rx[SWEEPS - 1, tc], axis=0)
        scales.append(1.0 / (row + (1.0 - live_ref[tc, 0])))
    own_scale = jnp.where(cc == 0, scales[0], scales[1])
    tall[0, 0] = own_scale * live
    tall[0, 1] = jnp.where(cc == 0, scales[1], scales[0]) * live_ref[1 - cc, 0]
    for k in range(1, NX):
        send_one(tall.at[0], tall.at[k], TOKENS, x_peers[k - 1])
        send_one(tall.at[0], tall.at[NX - 1 + k], TOKENS, y_peers[k - 1])
    t_b[...] = to_rows(own_scale * own_factor)
    fpt[...] = jnp.zeros(fpt.shape, jnp.float32)

    def own_block(table, v, h):
        base = column(v)
        some = pl.ds(h * TH, TH)
        for s in range(TILES):
            lanes = slice(s * 128, (s + 1) * 128)
            target = table[some, lanes] * t_b[some, :] * p_ref[pl.ds(v * TILES + s, 1), :]
            tgt[some, pl.ds(pl.multiple_of(base + s * 128, 128), 128)] = target.astype(jnp.bfloat16)
            delta_a[:TH, lanes] = (
                soft[v, some, lanes] * g_b[some, :] - target).astype(jnp.bfloat16)
        fpt[h] += lax.dot_general(
            w[v], delta_a[:TH, :], NT, preferred_element_type=jnp.float32
        ).reshape(fpt.shape[1:])

    def own_rows(h):
        def first_half(v, c):
            own_block(own.at[v], v, h)
            return c

        def second_half(v, c):
            own_block(rest.at[v], HALF + v, h)
            return c

        lax.fori_loop(0, HALF, first_half, 0)
        if h == 0:
            wait_all(p_ref.at[pl.ds(half_rows, half_rows)], recv.at[PHALF])
        lax.fori_loop(0, HALF, second_half, 0)
        for k in (4, 3, 5, 2, 6, 1, 7):
            send_one(fpt.at[h, z_place[k - 1]], f_rx.at[h, k - 1], FEATURE + h, z_peers[k - 1])

    def shared_part(q, c):
        rows = pl.ds(pl.multiple_of(q * 256, 256), 256)
        for a in range(2):
            for n in range(BLOCKS):
                for h in range(2):
                    lanes = slice(h * 128, (h + 1) * 128)
                    near = n % NX + (a * (NX - 1) if n % NX else 0)
                    target = (eb[a, n, rows, lanes] * pcol[a, rows, :]
                              * tall[near, n // NX, :, lanes])
                    dcat[:, n * ROWS + h * 128:n * ROWS + (h + 1) * 128] = (
                        qb[a, n, rows, lanes] - target).astype(jnp.bfloat16)
            grad = lax.dot_general(sft[a], dcat[...], NT, preferred_element_type=jnp.float32)
            for x in range(NX):
                for y in range(NY):
                    top = (x * NY + y) * 16
                    if a:
                        wp_tx[a, q, x, y * 16:(y + 1) * 16, :] = grad[top:top + 16]
                    else:
                        wp_tx[a, q, y, x * 16:(x + 1) * 16, :] = grad[top:top + 16]
            for k in (2, 1, 3):
                far = lax.rem(here[1 - a] + k, NX)
                send_one(wp_tx.at[a, q, far], rs_rx.at[a, q, k - 1], RS + a * SUBS + q,
                         axis_peers[1 - a][k - 1])
        return c

    own_rows(0)
    wait_all(tall.at[pl.ds(1, NX + NY - 2)], recv.at[TOKENS])
    lax.fori_loop(0, SUBS, shared_part, 0)
    own_rows(1)

    def collect(q, c):
        for a in range(2):
            wait_all(rs_rx.at[a, q], recv.at[RS + a * SUBS + q])
            grad = wp_tx[a, q, here[1 - a]] + jnp.sum(rs_rx[a, q], axis=0)
            a_tx[a, q] = grad.reshape(BLOCKS, 8, 256)
            for n in range(1, BLOCKS):
                far, core = place(a, n)
                send_one(a_tx.at[a, q, far * NC + core], a_rx.at[a, q, n - 1], SPREAD + a,
                         peer_of(a, n))
        return c

    lax.fori_loop(0, SUBS, collect, 0)
    for h in range(2):
        wait_all(f_rx.at[h], recv.at[FEATURE + h])
        feature_ref[:, h * TH:(h + 1) * TH] = fpt[h, z] + jnp.sum(f_rx[h], axis=0)
    for a in range(2):
        wait_all(a_rx.at[a], recv.at[SPREAD + a])
        for q in range(SUBS):
            for n in range(BLOCKS):
                far, core = source(a, n)
                span = pl.ds(pl.multiple_of(
                    core * HALF * WIDE + (a * NX + far) * THIN + q * 256, 256), 256)
                weight_ref[:, span] = a_rx[a, q, n - 1] if n else a_tx[a, q, here[a] * NC + cc]

    wait_all(gall.at[0, NX], send.at[PT])
    wait_all(gall.at[1, NX], send.at[PS])
    wait_all(live_ref.at[1 - cc], send.at[PM])
    wait_all(s_rx, send.at[TOTALS])
    for a in range(2):
        for t in range(2):
            wait_all(arrivals(a, t, 0), send.at[FEATS + 2 * a + t])
            wait_all(arrivals(a, t, 1), send.at[RELAY + 2 * a + t])
        wait_all(a_rx.at[a], send.at[SPREAD + a])
        wait_all(f_rx.at[a], send.at[FEATURE + a])
        for q in range(SUBS):
            wait_all(rs_rx.at[a, q], send.at[RS + a * SUBS + q])
    wait_all(scal.at[pl.ds(1, SLOTS - 1)], send.at[SCALARS])
    wait_all(tall.at[pl.ds(1, NX + NY - 2)], send.at[TOKENS])
    wait_all(k_rx, send.at[PEAK])
    wait_all(p_ref.at[pl.ds(half_rows, half_rows)], send.at[PHALF])
    for slot in range(SWEEPS):
        for tc in range(NC):
            wait_all(z_rx.at[slot, tc], send.at[ZS + 2 * slot + tc])
    for sweep in range(SWEEPS):
        for part in range(2):
            wait_all(x_rx.at[sweep, part], send.at[XS + 2 * sweep + part])
            wait_all(y_rx.at[sweep, part], send.at[YS + 2 * sweep + part])


def write_out(*refs):
    sems = refs[6]
    copies = [pltpu.make_async_copy(refs[i], refs[3 + i], sems.at[i]) for i in range(3)]
    for copy in copies:
        copy.start()
    for copy in copies:
        copy.wait()


def on_device(teacher_feats, student_feats, proto_weight, token_mask):
    d, protos = proto_weight.shape
    f32, bf16 = jnp.float32, jnp.bfloat16
    shared = pltpu.VMEM((2, BLOCKS, THIN, ROWS), f32)
    rows = pltpu.VMEM((ROWS, 128), f32)
    vmem = pl.BlockSpec(memory_space=pltpu.VMEM)
    hbm = pl.BlockSpec(memory_space=pl.ANY)
    results = pl.pallas_call(
        kernel,
        out_shape=(
            pltpu.VMEM((ROWS, protos), bf16),
            pltpu.VMEM((d // (NX * NY * NC), protos), f32),
            pltpu.VMEM((d // NZ, ROWS), f32),
        ),
        in_specs=[vmem, vmem, vmem, hbm],
        out_specs=(vmem, vmem, vmem),
        scratch_shapes=[
            pltpu.VMEM((BLOCKS, d, WIDE), bf16),
            pltpu.VMEM((NC, HALF, ROWS, WIDE), f32),
            pltpu.VMEM((HALF, ROWS, WIDE), f32),
            pltpu.VMEM((BLOCKS, ROWS, WIDE), f32),
            rows,
            pltpu.VMEM((NC, ROWS, 128), f32),
            rows, rows, rows,
            pltpu.VMEM((ROWS, WIDE), bf16),
            pltpu.VMEM((2, NZ, d // NZ, TH), f32),
            pltpu.VMEM((2, NZ - 1, d // NZ, TH), f32),
            pltpu.VMEM((2, THIN, d), bf16),
            shared, shared,
            pltpu.VMEM((2, SLOTS, d, ROWS), f32),
            pltpu.VMEM((2, d, BLOCKS * ROWS), bf16),
            pltpu.VMEM((256, BLOCKS * ROWS), bf16),
            pltpu.VMEM((2, THIN, 128), f32),
            pltpu.VMEM((SLOTS, 3, ROWS), f32),
            pltpu.VMEM((NX + NY - 1, NC, 1, ROWS), f32),
            pltpu.VMEM((2, SUBS, NX, d // NX, 256), f32),
            pltpu.VMEM((2, SUBS, NX - 1, d // NX, 256), f32),
            pltpu.VMEM((2, SUBS, BLOCKS, 8, 256), f32),
            pltpu.VMEM((2, SUBS, BLOCKS - 1, 8, 256), f32),
            pltpu.VMEM((NC, 2, 1, ROWS), f32),
            pltpu.VMEM((ZC, 1, ROWS), f32),
            pltpu.VMEM((2, LINE, 128), f32),
            pltpu.VMEM((SWEEPS, 2, LINE, 128), f32),
            pltpu.VMEM((SWEEPS, 2, NX - 1, LINE, 128), f32),
            pltpu.VMEM((SWEEPS, 2, LINE, 128), f32),
            pltpu.VMEM((SWEEPS, 2, NY - 1, LINE, 128), f32),
            pltpu.VMEM((BLOCKS * TILES, 128), f32),
            pltpu.VMEM((SWEEPS, NC, 1, ROWS), f32),
            pltpu.VMEM((SWEEPS, NC, ZC, 1, ROWS), f32),
            pltpu.VMEM((2, ROWS), f32),
            pltpu.VMEM((NZ - 1, 2, ROWS), f32),
            pltpu.SemaphoreType.DMA((BLOCKS,)),
            pltpu.SemaphoreType.DMA((GROUPS,)),
            pltpu.SemaphoreType.DMA((GROUPS,)),
        ],
        compiler_params=pltpu.CompilerParams(
            collective_id=0, has_side_effects=True, vmem_limit_bytes=58 * 2**20
        ),
        name="sinkhorn",
    )(teacher_feats, student_feats, token_mask.reshape(1, -1), proto_weight)
    targets, weight_grad, feature_grad = pl.pallas_call(
        write_out,
        out_shape=tuple(jax.ShapeDtypeStruct(r.shape, r.dtype) for r in results),
        in_specs=[hbm] * 3,
        out_specs=(hbm, hbm, hbm),
        scratch_shapes=[pltpu.SemaphoreType.DMA((3,))],
        compiler_params=pltpu.CompilerParams(vmem_limit_bytes=2**20),
        name="write_out",
    )(*results)
    return targets, weight_grad, feature_grad.T


def solution(mesh):
    placed = (P("dp", None), P("dp", None), P(None, "proto"), P("dp"))
    return jax.shard_map(
        on_device,
        mesh=mesh,
        in_specs=placed,
        out_specs=(P("dp", "proto"), P("dp", "proto"), P("dp", "proto")),
        check_vma=False,
    )
```

```python
import math

import jax
import jax.numpy as jnp
from jax import lax
from jax.experimental import pallas as pl
from jax.experimental.pallas import tpu as pltpu
from jax.sharding import PartitionSpec as P

SWEEPS = 3
TEACHER = math.log2(math.e) / 0.07
STUDENT = math.log2(math.e) / 0.1
MESH = pl.DeviceIdType.MESH
NX, NY, NC, NZ = 4, 4, 2, 8
ROWS = 256
WIDE = 1024
BLOCKS = 8
HALF = BLOCKS // 2
TILES = WIDE // 128
PARTS = WIDE // 256
THIN = WIDE // 2
SUBS = THIN // 256
SLOTS = 14
TH = ROWS // 2
LINE = HALF * TILES // 2
NT = (((1,), (1,)), ((), ()))
ZC = NZ * NC - 1
FIXED = 20
PT, PS, PM, TOTALS, SCALARS, TOKENS, PHALF, PEAK = range(8)
FEATS, RELAY, FEATURE, SPREAD = 8, 12, 16, 18
ZS = FIXED
XS = ZS + 2 * SWEEPS
YS = XS + 2 * SWEEPS
RS = YS + 2 * SWEEPS
GROUPS = RS + 2 * SUBS


def wait_all(ref, sem):
    pltpu.make_async_copy(ref, ref, sem).wait()


def to_rows(lanes, width=ROWS):
    return jnp.transpose(jnp.broadcast_to(lanes, (128, width)))


def kernel(
    tf_ref, sf_ref, mask_ref, w_hbm,
    tgt, weight_ref, feature_ref,
    w, expo, rest, soft, peak_b, acc, t_b, r_b, g_b, delta_a, fpt, f_rx,
    wt, eb, qb, gall, sft, dcat, pcol, scal, tall, wp_tx, rs_rx, a_tx, a_rx,
    live_ref, k_rx, col, x_tx, x_rx, y_tx, y_rx, p_ref,
    z_tx, z_rx, s_tx, s_rx,
    w_sem, send, recv,
):
    dp = lax.axis_index("dp")
    z = lax.axis_index("proto")
    cx, cy, cc = dp // (NY * NC), lax.rem(dp // NC, NY), lax.rem(dp, NC)

    def at(x, y, c):
        return {"dp": (x * NY + y) * NC + c}

    here = (cx, cy)

    def place(a, n):
        return lax.rem(here[a] + n % NX, NX), (cc if n < NX else 1 - cc)

    def source(a, n):
        return lax.rem(here[a] + NX - n % NX, NX), (cc if n < NX else 1 - cc)

    def peer_of(a, n):
        far, core = place(a, n)
        return at(cx, far, core) if a else at(far, cy, core)

    def slot_of(a, n):
        if a == 0 or n % NX == 0:
            return n
        return n + 7 if n < NX else n + 6

    partner = at(cx, cy, 1 - cc)
    shared_peers = [(slot_of(a, n), peer_of(a, n))
                    for a in range(2) for n in range(1, BLOCKS) if a == 0 or n != NX]
    x_peers = [peer_of(0, k) for k in range(1, NX)]
    y_peers = [peer_of(1, k) for k in range(1, NY)]
    axis_peers = (x_peers, y_peers)
    z_place = [lax.rem(z + k, NZ) for k in range(1, NZ)]
    z_peers = [{"proto": place} for place in z_place]
    zc_peers = z_peers + [partner] + [
        {"dp": dp + 1 - 2 * cc, "proto": place} for place in z_place]

    barrier = pltpu.get_barrier_semaphore()
    peers = [peer for _, peer in shared_peers] + z_peers + zc_peers[NZ:]
    for peer in peers:
        pl.semaphore_signal(barrier, inc=1, device_id=peer, device_id_type=MESH)

    def column(v):
        return pl.multiple_of(lax.rem(cc * HALF + v, BLOCKS) * WIDE, WIDE)

    def load(v):
        return pltpu.make_async_copy(w_hbm.at[:, pl.ds(column(v), WIDE)], w.at[v], w_sem.at[v])

    def start_load(v, c):
        load(v).start()
        return c

    lax.fori_loop(0, BLOCKS, start_load, 0)

    def send_one(src, dst, group, device):
        pltpu.make_async_remote_copy(
            src_ref=src, dst_ref=dst, send_sem=send.at[group], recv_sem=recv.at[group],
            device_id=device, device_id_type=MESH,
        ).start()

    def push(src, dst, group, devices):
        for k, device in enumerate(devices):
            send_one(src, dst.at[k], group, device)

    far_first = (12, 4, 11, 13, 3, 5, 10, 14, 2, 6, 9, 15, 1, 7, 8)

    def push_z(slot, tc):
        for n in far_first:
            send_one(z_tx.at[slot, tc], z_rx.at[slot, tc, n - 1], ZS + 2 * slot + tc,
                     zc_peers[n - 1])

    def wait_z(slot, tc):
        wait_all(z_rx.at[slot, tc], recv.at[ZS + 2 * slot + tc])

    def gather(a, first, last):
        for q in range(first, last):
            rows = pl.ds(q % 4 * 64, 64)
            for n in range(1, NX):
                send_one(gall.at[q // 4, 0, rows], gall.at[q // 4, slot_of(a, n), rows],
                         FEATS + 2 * a + q // 4, axis_peers[a][n - 1])

    def arrivals(a, t, core):
        return gall.at[t, pl.ds(slot_of(a, core * NX + 1), NX - 1)]

    def relay(t):
        for a in range(2):
            wait_all(arrivals(a, t, 0), recv.at[FEATS + 2 * a + t])
            send_one(arrivals(a, t, 0), arrivals(a, t, 1), RELAY + 2 * a + t, partner)

    def logits(feats, table, low, high, first):
        def block(v, c):
            if first:
                load(v).wait()
            part = jnp.dot(feats[...], w[v], preferred_element_type=jnp.float32)
            table[v - low] = part
            most = part[:, :128]
            for s in range(1, TILES):
                most = jnp.maximum(most, part[:, s * 128:(s + 1) * 128])
            acc[0] = jnp.maximum(acc[0], most)
            return c

        lax.fori_loop(low, high, block, 0)

    def no_peak():
        acc[0] = jnp.full(acc.shape[1:], -jnp.inf, jnp.float32)

    def found_peak():
        return jnp.max(jnp.transpose(acc[0]), axis=0, keepdims=True)

    def powers(table, peak, scale, blocks, total):
        def block(v, c):
            for s in range(TILES):
                at_s = (v, slice(None), slice(s * 128, (s + 1) * 128))
                value = jnp.exp2((table[at_s] - peak[...]) * scale)
                table[at_s] = value
                if total:
                    acc[0] += value
            return c

        lax.fori_loop(0, blocks, block, 0)

    def row_sum(tc):
        return jnp.sum(jnp.transpose(acc[tc]), axis=0, keepdims=True)

    def partner_table(feats, peak):
        def block(v, c):
            for s in range(PARTS):
                part = jnp.dot(
                    feats[...], w[v, :, s * 256:(s + 1) * 256],
                    preferred_element_type=jnp.float32,
                )
                for h in range(2):
                    others[v, :, s * 256 + h * 128:s * 256 + (h + 1) * 128] = jnp.exp2(
                        (part[:, h * 128:(h + 1) * 128] - peak[...]) * TEACHER)
            return c

        lax.fori_loop(0, HALF, block, 0)

    def shared_tables(t, places):
        for a in range(2):
            for n in places:
                slot = slot_of(a, n)
                feats = gall[t, slot].astype(jnp.bfloat16)
                if t:
                    sft[a, :, n * ROWS:(n + 1) * ROWS] = feats
                for q in range(SUBS):
                    rows = slice(q * 256, (q + 1) * 256)
                    dot = jnp.dot(wt[a, rows, :], feats, preferred_element_type=jnp.float32)
                    if t:
                        qb[a, n, rows, :] = jnp.exp2(
                            (dot - scal[slot, 1:2]) * STUDENT) * scal[slot, 2:3]
                    else:
                        eb[a, n, rows, :] = jnp.exp2((dot - scal[slot, 0:1]) * TEACHER)

    live = mask_ref[...].astype(jnp.float32)
    own = expo.at[cc]
    others = expo.at[1 - cc]
    gall[0, 0] = jnp.transpose(tf_ref[...].astype(jnp.float32))
    no_peak()
    logits(tf_ref, own, 0, HALF, True)
    logits(tf_ref, rest, HALF, BLOCKS, True)
    local_peak = found_peak()
    live_ref[cc, 0] = live
    live_ref[cc, 1] = local_peak
    pl.semaphore_wait(barrier, len(peers))
    for n in far_first:
        send_one(live_ref.at[cc, 1], k_rx.at[n - 1], PEAK, zc_peers[n - 1])
    send_one(gall.at[0, 0], gall.at[0, NX], PT, partner)
    send_one(live_ref.at[cc], live_ref.at[cc], PM, partner)
    gather(0, 0, 2)
    gather(1, 0, 3)
    r_b[...] = to_rows(local_peak)
    powers(own, r_b, TEACHER, HALF, False)
    wait_all(gall.at[0, NX], recv.at[PT])
    delta_a[:, :ROWS] = jnp.transpose(gall[0, NX].astype(jnp.bfloat16))
    wait_all(live_ref.at[1 - cc], recv.at[PM])
    t_b[...] = to_rows(live_ref[1 - cc, 1])
    partner_table(delta_a.at[:, pl.ds(0, ROWS)], t_b)
    gall[1, 0] = jnp.transpose(sf_ref[...].astype(jnp.float32))
    send_one(gall.at[1, 0], gall.at[1, NX], PS, partner)

    wait_all(k_rx, recv.at[PEAK])
    joint_peak = jnp.maximum(jnp.max(k_rx[:NZ - 1], axis=0), local_peak)
    own_factor = live * jnp.exp2((local_peak - joint_peak) * TEACHER)
    other_factor = live_ref[1 - cc, 0] * jnp.exp2(
        (live_ref[1 - cc, 1] - jnp.max(k_rx[NZ - 1:], axis=0)) * TEACHER)
    factors = [jnp.where(cc == tc, own_factor, other_factor) for tc in range(NC)]
    half_rows = HALF * TILES
    for sweep in range(SWEEPS):
        for tc in range(NC):
            scale = factors[tc]
            if sweep:
                wait_z(sweep - 1, tc)
                row = z_tx[sweep - 1, tc] + jnp.sum(z_rx[sweep - 1, tc], axis=0)
                scale = scale / (row + (1.0 - live_ref[tc, 0]))
            t_b[...] = to_rows(scale)
            for part in range(2):
                def column_block(v, c):
                    for s in range(TILES):
                        r = (v - part * (HALF // 2)) * TILES + s
                        total = jnp.sum(
                            expo[tc, v, :, s * 128:(s + 1) * 128] * t_b[...],
                            axis=0, keepdims=True)
                        if tc:
                            x_tx[sweep, part, pl.ds(r, 1), :] = (
                                col[part, pl.ds(r, 1), :] + total)
                        else:
                            col[part, pl.ds(r, 1), :] = total
                    return c

                lax.fori_loop(part * (HALF // 2), (part + 1) * (HALF // 2), column_block, 0)
                if tc:
                    group = XS + 2 * sweep + part
                    push(x_tx.at[sweep, part], x_rx.at[sweep, part], group, x_peers)

        if sweep == 0:
            no_peak()
            logits(sf_ref, soft, 0, BLOCKS, False)
            student_peak = found_peak()
            peak_b[...] = to_rows(student_peak)
        if sweep == 1:
            powers(rest, r_b, TEACHER, HALF, False)
        if sweep == 2:
            relay(1)
            for a in range(2):
                wait_all(arrivals(a, 0, 1), recv.at[RELAY + 2 * a])
            shared_tables(0, range(NX, BLOCKS))
        for part in range(2):
            wait_all(x_rx.at[sweep, part], recv.at[XS + 2 * sweep + part])
            y_tx[sweep, part] = x_tx[sweep, part] + jnp.sum(x_rx[sweep, part], axis=0)
            push(y_tx.at[sweep, part], y_rx.at[sweep, part], YS + 2 * sweep + part, y_peers)
        if sweep == 0:
            gather(0, 2, 5)
            acc[0] = jnp.zeros(acc.shape[1:], jnp.float32)
            powers(soft, peak_b, STUDENT, BLOCKS, True)
            student_total = row_sum(0)
            s_tx[0:1] = student_peak
            s_tx[1:2] = student_total
            push(s_tx, s_rx, TOTALS, z_peers)
        if sweep == 1:
            gather(0, 5, 8)
            relay(0)
        if sweep == 2:
            shared_tables(1, range(1, NX))
        acc[...] = jnp.zeros(acc.shape, jnp.float32)
        for part in range(2):
            wait_all(y_rx.at[sweep, part], recv.at[YS + 2 * sweep + part])
            p_ref[part * LINE:(part + 1) * LINE] = 1.0 / (
                y_tx[sweep, part] + jnp.sum(y_rx[sweep, part], axis=0))
            if part and sweep == SWEEPS - 1:
                send_one(p_ref.at[pl.ds(0, half_rows)], p_ref.at[pl.ds(half_rows, half_rows)],
                         PHALF, partner)
            for tc in range(NC):
                def row_block(v, c):
                    total = acc[tc]
                    for s in range(TILES):
                        total += (expo[tc, v, :, s * 128:(s + 1) * 128]
                                  * p_ref[pl.ds(v * TILES + s, 1), :])
                    acc[tc] = total
                    return c

                lax.fori_loop(part * (HALF // 2), (part + 1) * (HALF // 2), row_block, 0)
                if part:
                    z_tx[sweep, tc] = row_sum(tc) * factors[tc]
                    push_z(sweep, tc)
        if sweep == 0:
            gather(1, 3, 6)
            for a in range(2):
                lanes = pl.ds(pl.multiple_of(lax.rem(here[a], 2) * THIN, THIN), THIN)
                wt[a] = jnp.transpose(w[2 * a + here[a] // 2, :, lanes])
            wait_all(s_rx, recv.at[TOTALS])
            top = jnp.maximum(jnp.max(s_rx[:, 0:1], axis=0), student_peak)
            total = student_total * jnp.exp2((student_peak - top) * STUDENT)
            for k in range(NZ - 1):
                total += s_rx[k, 1:2] * jnp.exp2((s_rx[k, 0:1] - top) * STUDENT)
            share = live * jnp.exp2((student_peak - top) * STUDENT) / total
            g_b[...] = to_rows(share)
            scal[0, 0:1] = joint_peak
            scal[0, 1:2] = student_peak
            scal[0, 2:3] = share
            for slot, peer in shared_peers:
                send_one(scal.at[0], scal.at[slot], SCALARS, peer)
        if sweep == 1:
            gather(1, 6, 8)
            wait_all(scal.at[pl.ds(1, SLOTS - 1)], recv.at[SCALARS])
            wait_all(gall.at[1, NX], recv.at[PS])
            shared_tables(0, range(NX))
            shared_tables(1, (0, NX))
        if sweep == SWEEPS - 1:
            for a in range(2):
                wait_all(arrivals(a, 1, 1), recv.at[RELAY + 2 * a + 1])
            shared_tables(1, range(NX + 1, BLOCKS))
            for a in range(2):
                for s in range(TILES // 2):
                    line = a * LINE + here[a] * (TILES // 2) + s
                    pcol[a, s * 128:(s + 1) * 128, :] = to_rows(p_ref[pl.ds(line, 1), :], 128)

    scales = []
    for tc in range(NC):
        wait_z(SWEEPS - 1, tc)
        row = z_tx[SWEEPS - 1, tc] + jnp.sum(z_rx[SWEEPS - 1, tc], axis=0)
        scales.append(1.0 / (row + (1.0 - live_ref[tc, 0])))
    own_scale = jnp.where(cc == 0, scales[0], scales[1])
    tall[0, 0] = own_scale * live
    tall[0, 1] = jnp.where(cc == 0, scales[1], scales[0]) * live_ref[1 - cc, 0]
    for k in range(1, NX):
        send_one(tall.at[0], tall.at[k], TOKENS, x_peers[k - 1])
        send_one(tall.at[0], tall.at[NX - 1 + k], TOKENS, y_peers[k - 1])
    t_b[...] = to_rows(own_scale * own_factor)
    fpt[...] = jnp.zeros(fpt.shape, jnp.float32)

    def own_block(table, v, h):
        base = column(v)
        some = pl.ds(h * TH, TH)
        for s in range(TILES):
            lanes = slice(s * 128, (s + 1) * 128)
            target = table[some, lanes] * t_b[some, :] * p_ref[pl.ds(v * TILES + s, 1), :]
            tgt[some, pl.ds(pl.multiple_of(base + s * 128, 128), 128)] = target.astype(jnp.bfloat16)
            delta_a[:TH, lanes] = (
                soft[v, some, lanes] * g_b[some, :] - target).astype(jnp.bfloat16)
        fpt[h] += lax.dot_general(
            w[v], delta_a[:TH, :], NT, preferred_element_type=jnp.float32
        ).reshape(fpt.shape[1:])

    def own_rows(h, early):
        def first_half(v, c):
            own_block(own.at[v], v, h)
            return c

        def second_half(v, c):
            own_block(rest.at[v], HALF + v, h)
            return c

        if h or early:
            lax.fori_loop(0, HALF, first_half, 0)
        if early:
            return
        if h == 0:
            wait_all(p_ref.at[pl.ds(half_rows, half_rows)], recv.at[PHALF])
        lax.fori_loop(0, HALF, second_half, 0)
        for k in (4, 3, 5, 2, 6, 1, 7):
            send_one(fpt.at[h, z_place[k - 1]], f_rx.at[h, k - 1], FEATURE + h, z_peers[k - 1])

    def shared_part(q, c):
        rows = pl.ds(pl.multiple_of(q * 256, 256), 256)
        for a in range(2):
            for n in range(BLOCKS):
                for h in range(2):
                    lanes = slice(h * 128, (h + 1) * 128)
                    near = n % NX + (a * (NX - 1) if n % NX else 0)
                    target = (eb[a, n, rows, lanes] * pcol[a, rows, :]
                              * tall[near, n // NX, :, lanes])
                    dcat[:, n * ROWS + h * 128:n * ROWS + (h + 1) * 128] = (
                        qb[a, n, rows, lanes] - target).astype(jnp.bfloat16)
            grad = lax.dot_general(sft[a], dcat[...], NT, preferred_element_type=jnp.float32)
            for x in range(NX):
                for y in range(NY):
                    top = (x * NY + y) * 16
                    if a:
                        wp_tx[a, q, x, y * 16:(y + 1) * 16, :] = grad[top:top + 16]
                    else:
                        wp_tx[a, q, y, x * 16:(x + 1) * 16, :] = grad[top:top + 16]
            for k in (2, 1, 3):
                far = lax.rem(here[1 - a] + k, NX)
                send_one(wp_tx.at[a, q, far], rs_rx.at[a, q, k - 1], RS + a * SUBS + q,
                         axis_peers[1 - a][k - 1])
        return c

    own_rows(0, True)
    wait_all(tall.at[pl.ds(1, NX + NY - 2)], recv.at[TOKENS])
    lax.fori_loop(0, SUBS, shared_part, 0)
    own_rows(0, False)
    own_rows(1, False)

    def collect(q, c):
        for a in range(2):
            wait_all(rs_rx.at[a, q], recv.at[RS + a * SUBS + q])
            grad = wp_tx[a, q, here[1 - a]] + jnp.sum(rs_rx[a, q], axis=0)
            a_tx[a, q] = grad.reshape(BLOCKS, 8, 256)
            for n in (6, 2, 5, 7, 1, 3, 4):
                far, core = place(a, n)
                send_one(a_tx.at[a, q, far * NC + core], a_rx.at[a, q, n - 1], SPREAD + a,
                         peer_of(a, n))
        return c

    lax.fori_loop(0, SUBS, collect, 0)
    for h in range(2):
        wait_all(f_rx.at[h], recv.at[FEATURE + h])
        feature_ref[:, h * TH:(h + 1) * TH] = fpt[h, z] + jnp.sum(f_rx[h], axis=0)
    for a in range(2):
        wait_all(a_rx.at[a], recv.at[SPREAD + a])
        for q in range(SUBS):
            for n in range(BLOCKS):
                far, core = source(a, n)
                span = pl.ds(pl.multiple_of(
                    core * HALF * WIDE + (a * NX + far) * THIN + q * 256, 256), 256)
                weight_ref[:, span] = a_rx[a, q, n - 1] if n else a_tx[a, q, here[a] * NC + cc]

    wait_all(gall.at[0, NX], send.at[PT])
    wait_all(gall.at[1, NX], send.at[PS])
    wait_all(live_ref.at[1 - cc], send.at[PM])
    wait_all(s_rx, send.at[TOTALS])
    for a in range(2):
        for t in range(2):
            wait_all(arrivals(a, t, 0), send.at[FEATS + 2 * a + t])
            wait_all(arrivals(a, t, 1), send.at[RELAY + 2 * a + t])
        wait_all(a_rx.at[a], send.at[SPREAD + a])
        wait_all(f_rx.at[a], send.at[FEATURE + a])
        for q in range(SUBS):
            wait_all(rs_rx.at[a, q], send.at[RS + a * SUBS + q])
    wait_all(scal.at[pl.ds(1, SLOTS - 1)], send.at[SCALARS])
    wait_all(tall.at[pl.ds(1, NX + NY - 2)], send.at[TOKENS])
    wait_all(k_rx, send.at[PEAK])
    wait_all(p_ref.at[pl.ds(half_rows, half_rows)], send.at[PHALF])
    for slot in range(SWEEPS):
        for tc in range(NC):
            wait_all(z_rx.at[slot, tc], send.at[ZS + 2 * slot + tc])
    for sweep in range(SWEEPS):
        for part in range(2):
            wait_all(x_rx.at[sweep, part], send.at[XS + 2 * sweep + part])
            wait_all(y_rx.at[sweep, part], send.at[YS + 2 * sweep + part])


def write_out(*refs):
    sems = refs[6]
    copies = [pltpu.make_async_copy(refs[i], refs[3 + i], sems.at[i]) for i in range(3)]
    for copy in copies:
        copy.start()
    for copy in copies:
        copy.wait()


def on_device(teacher_feats, student_feats, proto_weight, token_mask):
    d, protos = proto_weight.shape
    f32, bf16 = jnp.float32, jnp.bfloat16
    shared = pltpu.VMEM((2, BLOCKS, THIN, ROWS), f32)
    rows = pltpu.VMEM((ROWS, 128), f32)
    vmem = pl.BlockSpec(memory_space=pltpu.VMEM)
    hbm = pl.BlockSpec(memory_space=pl.ANY)
    results = pl.pallas_call(
        kernel,
        out_shape=(
            pltpu.VMEM((ROWS, protos), bf16),
            pltpu.VMEM((d // (NX * NY * NC), protos), f32),
            pltpu.VMEM((d // NZ, ROWS), f32),
        ),
        in_specs=[vmem, vmem, vmem, hbm],
        out_specs=(vmem, vmem, vmem),
        scratch_shapes=[
            pltpu.VMEM((BLOCKS, d, WIDE), bf16),
            pltpu.VMEM((NC, HALF, ROWS, WIDE), f32),
            pltpu.VMEM((HALF, ROWS, WIDE), f32),
            pltpu.VMEM((BLOCKS, ROWS, WIDE), f32),
            rows,
            pltpu.VMEM((NC, ROWS, 128), f32),
            rows, rows, rows,
            pltpu.VMEM((ROWS, WIDE), bf16),
            pltpu.VMEM((2, NZ, d // NZ, TH), f32),
            pltpu.VMEM((2, NZ - 1, d // NZ, TH), f32),
            pltpu.VMEM((2, THIN, d), bf16),
            shared, shared,
            pltpu.VMEM((2, SLOTS, d, ROWS), f32),
            pltpu.VMEM((2, d, BLOCKS * ROWS), bf16),
            pltpu.VMEM((256, BLOCKS * ROWS), bf16),
            pltpu.VMEM((2, THIN, 128), f32),
            pltpu.VMEM((SLOTS, 3, ROWS), f32),
            pltpu.VMEM((NX + NY - 1, NC, 1, ROWS), f32),
            pltpu.VMEM((2, SUBS, NX, d // NX, 256), f32),
            pltpu.VMEM((2, SUBS, NX - 1, d // NX, 256), f32),
            pltpu.VMEM((2, SUBS, BLOCKS, 8, 256), f32),
            pltpu.VMEM((2, SUBS, BLOCKS - 1, 8, 256), f32),
            pltpu.VMEM((NC, 2, 1, ROWS), f32),
            pltpu.VMEM((ZC, 1, ROWS), f32),
            pltpu.VMEM((2, LINE, 128), f32),
            pltpu.VMEM((SWEEPS, 2, LINE, 128), f32),
            pltpu.VMEM((SWEEPS, 2, NX - 1, LINE, 128), f32),
            pltpu.VMEM((SWEEPS, 2, LINE, 128), f32),
            pltpu.VMEM((SWEEPS, 2, NY - 1, LINE, 128), f32),
            pltpu.VMEM((BLOCKS * TILES, 128), f32),
            pltpu.VMEM((SWEEPS, NC, 1, ROWS), f32),
            pltpu.VMEM((SWEEPS, NC, ZC, 1, ROWS), f32),
            pltpu.VMEM((2, ROWS), f32),
            pltpu.VMEM((NZ - 1, 2, ROWS), f32),
            pltpu.SemaphoreType.DMA((BLOCKS,)),
            pltpu.SemaphoreType.DMA((GROUPS,)),
            pltpu.SemaphoreType.DMA((GROUPS,)),
        ],
        compiler_params=pltpu.CompilerParams(
            collective_id=0, has_side_effects=True, vmem_limit_bytes=58 * 2**20
        ),
        name="sinkhorn",
    )(teacher_feats, student_feats, token_mask.reshape(1, -1), proto_weight)
    targets, weight_grad, feature_grad = pl.pallas_call(
        write_out,
        out_shape=tuple(jax.ShapeDtypeStruct(r.shape, r.dtype) for r in results),
        in_specs=[hbm] * 3,
        out_specs=(hbm, hbm, hbm),
        scratch_shapes=[pltpu.SemaphoreType.DMA((3,))],
        compiler_params=pltpu.CompilerParams(vmem_limit_bytes=2**20),
        name="write_out",
    )(*results)
    return targets, weight_grad, feature_grad.T


def solution(mesh):
    placed = (P("dp", None), P("dp", None), P(None, "proto"), P("dp"))
    return jax.shard_map(
        on_device,
        mesh=mesh,
        in_specs=placed,
        out_specs=(P("dp", "proto"), P("dp", "proto"), P("dp", "proto")),
        check_vma=False,
    )
```
